256 devices in a mesh: depth: 16 (over y, x), row: 8 (over z), col: 2 (over core).
Axes of the slice: x: 4, y: 4, z: 8, core: 2. Of those that a mesh axis runs over, the one named last changes fastest.
Arguments:
- inputs: bfloat16 [2048, 6144], P(('depth', 'col'), 'row'), may hold values from -6 to 6
- weight: bfloat16 [2, 6144, 12288], P('col', 'row', 'depth'), may hold values from -0.078125 to 0.078125
- cotangent: bfloat16 [2048, 24576], P(('depth', 'row'), 'col'), may hold values from -6 to 6
Outputs:
- activations: bfloat16 [2048, 24576], P(('depth', 'row'), 'col')
- grad_input: bfloat16 [2048, 6144], P(('depth', 'col'), 'row')
- grad_weight: float32 [2, 6144, 12288], P('col', 'row', 'depth')
The draws below stay inside these ranges and needn't reach their ends.
All inputs are finite; a program needn't handle non-finite values.
Results may differ from the reference program's by a relative error of at most 0.005.
Values may be sent and summed in bfloat16 or wider, within the bound.
A program may use at most 128 MiB of HBM per device.

```python
import math
import jax
import jax.numpy as jnp
from jax import lax

D = 6144
F = 24576
TOKENS = 2048
N_COL = 2


def steps_of(stream_key, extent, pieces, smallest, high):
    def one(position, shards_of):
        draws = jax.random.uniform(jax.random.fold_in(jax.random.fold_in(stream_key, 6), position), (shards_of,), jnp.float32, smallest / len(pieces), high / len(pieces))
        return jnp.repeat(jnp.exp(draws), extent[position] // shards_of).reshape((-1,) + (1,) * (len(extent) - position - 1))

    factor_of = one(*pieces[0])
    for cut in pieces[1:]:
        factor_of = factor_of * one(*cut)
    return factor_of


def noise(stream_key, dims, scale, reach, split=(), kind=jnp.bfloat16):
    result = jax.random.normal(stream_key, dims, jnp.float32) * scale
    if len(split) > 0:
        result = steps_of(stream_key, dims, split, -0.22, 0.18) * result
    return jnp.clip(result, min=-reach, max=reach).astype(kind)


def setup_inputs(seed: int = 0) -> dict:
    splits = jax.random.split(jax.random.key(seed), 4)
    return {
        "inputs": noise(splits[0], (TOKENS, D), 1.0, 6.0, ((0, 32), (1, 8))),
        "weight": noise(splits[1], (N_COL, D, F // N_COL), D ** -0.5, 0.078125, ((0, 2), (1, 8), (2, 16))),
        "cotangent": noise(splits[2], (TOKENS, F), 1.0, 6.0, ((0, 128), (1, 2))),
    }


slope_c = math.sqrt(2.0 / math.pi)

def gelu_value(h):
    u = slope_c * (h + 0.044715 * h * h * h)
    return 0.5 * h * (1.0 + jnp.tanh(u))

def gelu_slope(h):
    t = jnp.tanh(slope_c * (h + 0.044715 * h * h * h))
    return 0.5 * (1.0 + t) + 0.5 * h * (1.0 - t * t) * slope_c * (1.0 + 3.0 * 0.044715 * h * h)

def reference(inputs, weight, cotangent):
    blocks = weight.shape[0]
    matrix = jnp.transpose(weight, (1, 0, 2)).reshape(D, F)
    hidden = jnp.dot(inputs, matrix, preferred_element_type=jnp.float32)
    activations = gelu_value(hidden).astype(jnp.bfloat16)
    grad_hidden = (cotangent.astype(jnp.float32) * gelu_slope(hidden)).astype(jnp.bfloat16)
    grad_input = lax.dot_general(grad_hidden, matrix, (((1,), (1,)), ((), ())), preferred_element_type=jnp.float32).astype(jnp.bfloat16)
    factor = 1.0 / math.sqrt(TOKENS)
    grad_full = lax.dot_general(inputs, grad_hidden, (((0,), (0,)), ((), ())), preferred_element_type=jnp.float32) * factor
    grad_weight = jnp.transpose(grad_full.reshape(D, blocks, F // blocks), (1, 0, 2))
    return (activations, grad_input, grad_weight)
```

```python
import math

import jax
import jax.numpy as jnp
from jax import lax
from jax.sharding import PartitionSpec as P

slope_c = math.sqrt(2.0 / math.pi)


def gelu_both(h):
    t = jnp.tanh(slope_c * (h + 0.044715 * h * h * h))
    value = 0.5 * h * (1.0 + t)
    slope = 0.5 * (1.0 + t) + 0.5 * h * (1.0 - t * t) * slope_c * (1.0 + 3.0 * 0.044715 * h * h)
    return value, slope


def local(inputs, weight, cotangent):
    w = weight[0]
    rows, depths = lax.axis_size("row"), lax.axis_size("depth")
    x_all = lax.all_gather(inputs, ("depth", "col"), axis=0, tiled=True)
    tokens, width = x_all.shape
    own = tokens // (rows * depths)
    cot = lax.all_to_all(cotangent, "depth", split_axis=1, concat_axis=0, tiled=True)
    x_rows = x_all.reshape(depths, rows, own, width).transpose(1, 0, 2, 3).reshape(tokens, width)
    terms = jnp.dot(x_rows, w, preferred_element_type=jnp.float32)
    hidden = lax.psum_scatter(terms, "row", scatter_dimension=0, tiled=True)
    value, slope = gelu_both(hidden)
    activations = lax.all_to_all(
        value.astype(jnp.bfloat16), "depth", split_axis=0, concat_axis=1, tiled=True
    )
    grad_share = (cot.astype(jnp.float32) * slope).astype(jnp.bfloat16)
    grad_rows = lax.all_gather(grad_share, "row", axis=0, tiled=True)
    partial_input = lax.dot_general(
        grad_rows, w, (((1,), (1,)), ((), ())), preferred_element_type=jnp.float32
    )
    partial_input = partial_input.reshape(rows, depths, own, width).transpose(1, 0, 2, 3)
    grad_input = lax.psum_scatter(
        partial_input.reshape(tokens, width), ("depth", "col"), scatter_dimension=0, tiled=True
    ).astype(jnp.bfloat16)
    factor = 1.0 / math.sqrt(tokens)
    grad_local = (
        lax.dot_general(
            x_rows, grad_rows, (((0,), (0,)), ((), ())), preferred_element_type=jnp.float32
        )
        * factor
    )
    return (activations, grad_input, grad_local[None])


def solution(mesh):
    in_specs = (P(("depth", "col"), "row"), P("col", "row", "depth"), P(("depth", "row"), "col"))
    out_specs = (P(("depth", "row"), "col"), P(("depth", "col"), "row"), P("col", "row", "depth"))
    return jax.shard_map(local, mesh=mesh, in_specs=in_specs, out_specs=out_specs, check_vma=False)
```

```python
import functools
import math

import jax
import jax.numpy as jnp
from jax import lax
from jax.experimental import pallas as pl
from jax.experimental.pallas import tpu as pltpu
from jax.sharding import PartitionSpec as P

MESH = pl.DeviceIdType.MESH
slope_c = math.sqrt(2.0 / math.pi)
bf16, f32 = jnp.bfloat16, jnp.float32
NY, NX, NZ, NC = 4, 4, 8, 2
OWN = 16
WIDTH = 768
HALF = WIDTH // 2
TILE = 256

SLOTS = (
    (0, 0), (1, 0), (3, 0), (0, 2), (1, 1), (1, 3), (3, 1), (3, 3),
    (2, 0), (1, 2), (3, 2), (2, 1), (2, 3), (2, 2), (0, 1), (0, 3),
)
CHUNKS = (
    (0, 1), (1, 2), (3, 3), (6, 4), (10, 4), (14, 2),
)
COPIES = 228
ORDER = (
    ("s",), ("k", 1), ("k", 0), ("k", 2), ("k", 3), ("m", 0),
    ("r", 0, 0), ("x", 0, 3), ("x", 3, 0), ("x", 1, 0), ("x", 0, 1), ("r", 0, 1),
    ("m", 1), ("r", 0, 2), ("r", 1, 0), ("m", 5), ("x", 3, 3), ("r", 5, 0),
    ("r", 0, 3), ("r", 1, 1), ("r", 5, 1), ("x", 0, 2), ("x", 3, 1), ("f", 0),
    ("x", 1, 3), ("r", 1, 2), ("x", 2, 0), ("r", 5, 2), ("g", 0, 1), ("x", 3, 2),
    ("x", 1, 1), ("r", 1, 3), ("r", 5, 3), ("m", 2), ("g", 0, 2), ("x", 1, 2),
    ("r", 2, 0), ("x", 2, 3), ("f", 1), ("x", 2, 1), ("f", 5), ("g", 0, 3),
    ("m", 3), ("x", 2, 2), ("r", 2, 1), ("g", 1, 1), ("r", 3, 0), ("g", 5, 1),
    ("m", 4), ("b", 0), ("r", 4, 0), ("r", 2, 2), ("g", 1, 2), ("d", 0),
    ("r", 3, 1), ("g", 5, 2), ("r", 4, 1), ("r", 2, 3), ("g", 1, 3), ("r", 3, 2),
    ("g", 5, 3), ("r", 4, 2), ("f", 2), ("b", 1), ("r", 3, 3), ("b", 5),
    ("d", 1), ("r", 4, 3), ("d", 5), ("g", 2, 1), ("f", 3), ("f", 4),
    ("g", 2, 2), ("g", 3, 1), ("g", 4, 1), ("g", 2, 3), ("g", 3, 2), ("g", 4, 2),
    ("b", 2), ("g", 3, 3), ("d", 2), ("e", 0), ("g", 4, 3), ("b", 3),
    ("h", 0, 1), ("b", 4), ("h", 0, 0), ("w", 0, 8, True, False), ("d", 4), ("e", 2),
    ("d", 3), ("e", 1), ("e", 3), ("w", 8, 6, False, False), ("j", 0), ("h", 2, 0),
    ("h", 2, 1), ("w", 14, 2, False, True), ("h", 1, 0), ("h", 1, 1), ("h", 3, 1), ("h", 3, 0),
    ("j", 2), ("u",), ("j", 1), ("v", 0), ("j", 3), ("v", 1),
    ("z",),
)
SLOT = {name: index for index, name in enumerate(SLOTS)}


def gelu_both(h):
    t = jnp.tanh(slope_c * (h + 0.044715 * h * h * h))
    value = 0.5 * h * (1.0 + t)
    slope = 0.5 * (1.0 + t) + 0.5 * h * (1.0 - t * t) * slope_c * (1.0 + 3.0 * 0.044715 * h * h)
    return value, slope


def kernel(
    factor, x_in, w, cot_in, act_out, dx_out, gw_out,
    xs, gh, cot, part, ring_out, ring_in, act, swap_out, swap_in, x_out, x_got, total, y_out, y_got,
    send_sem, recv_sem, local_sem,
):
    depth, row, col = lax.axis_index("depth"), lax.axis_index("row"), lax.axis_index("col")
    y, x = depth // NX, lax.rem(depth, NX)

    def at_depth(dy, dx):
        return lax.rem(y + dy, NY) * NX + lax.rem(x + dx, NX)

    def near(dy, dx):
        return (at_depth(dy, dx), row, col)

    z_near = ((depth, lax.rem(row + 1, NZ), col), (depth, lax.rem(row + NZ - 1, NZ), col))
    x_near = (near(0, 1), near(0, 3))
    y_near = (near(1, 0), near(3, 0))
    other = (depth, row, 1 - col)
    offsets = [(dy, dx) for dy in range(NY) for dx in range(NX) if (dy, dx) != (0, 0)]

    copies, index_of = {}, {}

    def copy(name, src, dst, device):
        index = len(index_of)
        index_of[name] = index
        made = pltpu.make_async_remote_copy(
            src_ref=src, dst_ref=dst, send_sem=send_sem.at[index], recv_sem=recv_sem.at[index],
            device_id=device, device_id_type=MESH,
        )
        copies[name] = made
        made.start()

    def arrived(name):
        copies[name].wait_recv()

    def each(count, body):
        def step(j, carry):
            body(j)
            return carry
        lax.fori_loop(0, count, step, 0)

    mine = pl.multiple_of(col * 4, 4)
    theirs = pl.multiple_of(4 - col * 4, 4)

    def inputs_to_core(slot):
        block = xs.at[slot, pl.ds(mine, 4)]
        copy(("xc", slot), block, block, other)

    def start():
        barrier = pltpu.get_barrier_semaphore()
        peers = [near(*o) for o in offsets] + [other, *z_near]
        for peer in peers:
            pl.semaphore_signal(barrier, inc=1, device_id=peer, device_id_type=MESH)
        own = pltpu.make_async_copy(x_in, xs.at[SLOT[0, 0], pl.ds(mine, 4)], local_sem.at[0])
        own.start()
        own_cot = pltpu.make_async_copy(
            cot_in.at[:, pl.ds(pl.multiple_of(depth * WIDTH, WIDTH), WIDTH)],
            cot.at[SLOT[0, 0]], local_sem.at[1],
        )
        own_cot.start()
        own.wait()
        own_cot.wait()
        pl.semaphore_wait(barrier, len(peers))
        for (dy, dx), device in (((0, 3), x_near[0]), ((0, 1), x_near[1]), ((3, 0), y_near[0]), ((1, 0), y_near[1])):
            copy(("x", dy, dx), x_in, xs.at[SLOT[dy, dx], pl.ds(mine, 4)], device)
        copy(("xc", SLOT[0, 0]), x_in, xs.at[SLOT[0, 0], pl.ds(mine, 4)], other)

    def half_of(slot, half):
        return xs.at[slot, pl.ds(pl.multiple_of(col * 4 + 2 * half, 2), 2)]

    def gather(dy, dx):
        slot = SLOT[dy, dx]
        whole = xs.at[slot, pl.ds(mine, 4)]
        if dx == 2 and dy == 0 or dy == 2:
            arrived(("xh", dy, dx, 0))
            arrived(("xh", dy, dx, 1))
        else:
            arrived(("x", dy, dx))
        if dy == 0:
            if dx == 3:
                copy(("xh", 0, 2, 0), half_of(slot, 0), half_of(SLOT[0, 2], 0), x_near[0])
            if dx == 1:
                copy(("xh", 0, 2, 1), half_of(slot, 1), half_of(SLOT[0, 2], 1), x_near[1])
            copy(("x", 3, dx), whole, xs.at[SLOT[3, dx], pl.ds(mine, 4)], y_near[0])
            copy(("x", 1, dx), whole, xs.at[SLOT[1, dx], pl.ds(mine, 4)], y_near[1])
        if dy == 3:
            copy(("xh", 2, dx, 0), half_of(slot, 0), half_of(SLOT[2, dx], 0), y_near[0])
        if dy == 1:
            copy(("xh", 2, dx, 1), half_of(slot, 1), half_of(SLOT[2, dx], 1), y_near[1])
        inputs_to_core(slot)

    def spread_cot(dy):
        for dx in range(NX):
            if (dy, dx) != (0, 0):
                block = cot_in.at[:, pl.ds(pl.multiple_of(at_depth(dy, dx) * WIDTH, WIDTH), WIDTH)]
                slot = SLOT[(4 - dy) % 4, (4 - dx) % 4]
                copy(("k", slot), block, cot.at[slot], near(dy, dx))

    def forward(c):
        first, count = CHUNKS[c]
        for slot in range(first, first + count):
            arrived(("xc", slot))
        block = xs[first : first + count].reshape(count * NZ * OWN, WIDTH)

        def tile(j):
            columns = pl.ds(pl.multiple_of(j * TILE, TILE), TILE)
            terms = jnp.dot(block, w[:, columns], preferred_element_type=f32)
            part[first : first + count, :, :, columns] = terms.reshape(count, NZ, OWN, TILE)

        each(WIDTH // TILE, tile)

    def scatter(c, step):
        first, count = CHUNKS[c]
        slots = pl.ds(first, count)
        for way in range(2):
            owner = lax.rem(row + (4 - step if way == 0 else 4 + step), NZ)
            halves = (slice(0, HALF), slice(HALF, WIDTH))
            if step > 0:
                arrived(("r", c, step - 1, way))

            def add(j):
                s = first + j
                if step == 0:
                    cols = halves[way]
                    ring_out[way, 0, s, :, cols] = part[s, owner, :, cols].astype(bf16)
                elif step == 1:
                    cols, rest = halves[way], halves[1 - way]
                    got = ring_in[way, 0, s, :, cols].astype(f32)
                    ring_out[way, 1, s, :, cols] = (part[s, owner, :, cols] + got).astype(bf16)
                    ring_out[way, 1, s, :, rest] = part[s, owner, :, rest].astype(bf16)
                else:
                    got = ring_in[way, step - 1, s].astype(f32)
                    ring_out[way, step, s] = (part[s, owner] + got).astype(bf16)

            each(count, add)
            cols = halves[way] if step == 0 else slice(0, WIDTH)
            copy(
                ("r", c, step, way), ring_out.at[way, step, slots, :, cols],
                ring_in.at[way, step, slots, :, cols], z_near[way],
            )

    def activate(c):
        first, count = CHUNKS[c]
        arrived(("r", c, 3, 0))
        arrived(("r", c, 3, 1))
        for slot in range(first, first + count):
            if slot != SLOT[0, 0]:
                arrived(("k", slot))

        def one(j):
            s = first + j
            h = part[s, row] + ring_in[0, 3, s].astype(f32) + ring_in[1, 3, s].astype(f32)
            value, slope = gelu_both(h)
            act[s] = value.astype(bf16)
            gh[s, row] = (cot[s].astype(f32) * slope).astype(bf16)

        each(count, one)
        spread(c, 0)
        here = pl.ds(pl.multiple_of(depth * WIDTH, WIDTH), WIDTH)
        for slot in range(first, first + count):
            if slot == SLOT[0, 0]:
                own = pltpu.make_async_copy(act.at[slot], act_out.at[:, here], local_sem.at[2])
                own.start()
                own.wait()
            else:
                copy(("a", slot), act.at[slot], act_out.at[:, here], near(*SLOTS[slot]))

    def spread(c, step):
        first, count = CHUNKS[c]
        slots = pl.ds(first, count)
        for way in range(2):
            if step > 0:
                arrived(("g", c, step - 1, way))
            owner = lax.rem(row + (NZ - step if way == 0 else step), NZ)
            cols = slice(0, WIDTH) if step < 3 else (slice(0, HALF), slice(HALF, WIDTH))[way]
            block = gh.at[slots, owner, :, cols]
            copy(("g", c, step, way), block, block, z_near[way])

    def input_terms(c):
        first, count = CHUNKS[c]
        arrived(("g", c, 3, 0))
        arrived(("g", c, 3, 1))
        block = gh[first : first + count].reshape(count * NZ * OWN, WIDTH)

        def tile(j):
            features = pl.ds(pl.multiple_of(j * TILE, TILE), TILE)
            terms = lax.dot_general(
                block, w[features, :], (((1,), (1,)), ((), ())), preferred_element_type=f32
            )
            part[first : first + count, :, :, features] = terms.reshape(count, NZ, OWN, TILE)

        each(WIDTH // TILE, tile)

        def pick(j):
            swap_out[first + j] = part[first + j, pl.ds(theirs, 4)].astype(bf16)

        each(count, pick)
        slots = pl.ds(first, count)
        copy(("d", c), swap_out.at[slots], swap_in.at[slots], other)

    def weight_terms(first, count, is_first, is_last):
        def tile(j):
            features = pl.ds(pl.multiple_of(j * TILE, TILE), TILE)
            tokens = xs[first : first + count, :, :, features].reshape(count * NZ * OWN, TILE)
            grads = gh[first : first + count].reshape(count * NZ * OWN, WIDTH)
            terms = lax.dot_general(
                tokens, grads, (((0,), (0,)), ((), ())), preferred_element_type=f32
            )
            if not is_first:
                terms = terms + gw_out[features, :]
            if is_last:
                terms = terms * factor
            gw_out[features, :] = terms

        each(WIDTH // TILE, tile)

    def both(slot, j):
        return part[slot, mine + j] + swap_in[slot, j].astype(f32)

    def swapped(c):
        arrived(("d", c))

    def x_first(dy):
        slot = SLOT[dy, 2]

        def one(j):
            x_out[dy, j // 2, 0, j] = both(slot, j).astype(bf16)

        each(4, one)
        for way in range(2):
            rows = pl.ds(2 * way, 2)
            copy(("e", dy, 0, way), x_out.at[dy, way, 0, rows], x_got.at[dy, way, 0, rows], x_near[way])

    def x_second(dy, way):
        slot = SLOT[dy, (1, 3)[way]]
        arrived(("e", dy, 0, way))

        def with_got(j):
            j = j + 2 * way
            x_out[dy, way, 1, j] = (both(slot, j) + x_got[dy, way, 0, j].astype(f32)).astype(bf16)

        def without(j):
            j = j + 2 * (1 - way)
            x_out[dy, way, 1, j] = both(slot, j).astype(bf16)

        each(2, with_got)
        each(2, without)
        copy(("e", dy, 1, way), x_out.at[dy, way, 1], x_got.at[dy, way, 1], x_near[way])

    def x_last(dy):
        slot = SLOT[dy, 0]
        arrived(("e", dy, 1, 0))
        arrived(("e", dy, 1, 1))

        def one(j):
            total[dy, j] = (
                both(slot, j) + x_got[dy, 0, 1, j].astype(f32) + x_got[dy, 1, 1, j].astype(f32)
            )

        each(4, one)

    def y_first():
        def one(j):
            y_out[j // 2, 0, j] = total[2, j].astype(bf16)

        each(4, one)
        for way in range(2):
            rows = pl.ds(2 * way, 2)
            copy(("y", 0, way), y_out.at[way, 0, rows], y_got.at[way, 0, rows], y_near[way])

    def y_second(way):
        arrived(("y", 0, way))

        def with_got(j):
            j = j + 2 * way
            y_out[way, 1, j] = (total[(1, 3)[way], j] + y_got[way, 0, j].astype(f32)).astype(bf16)

        def without(j):
            j = j + 2 * (1 - way)
            y_out[way, 1, j] = total[(1, 3)[way], j].astype(bf16)

        each(2, with_got)
        each(2, without)
        copy(("y", 1, way), y_out.at[way, 1], y_got.at[way, 1], y_near[way])

    def y_last():
        arrived(("y", 1, 0))
        arrived(("y", 1, 1))

        def one(j):
            dx_out[j] = (
                total[0, j] + y_got[0, 1, j].astype(f32) + y_got[1, 1, j].astype(f32)
            ).astype(bf16)

        each(4, one)

    actions = dict(
        s=start, x=gather, k=spread_cot, m=forward, r=scatter, f=activate, g=spread, b=input_terms,
        w=weight_terms, d=swapped, e=x_first, h=x_second, j=x_last, u=y_first, v=y_second, z=y_last,
    )
    for event in ORDER:
        actions[event[0]](*event[1:])
    for slot in range(1, len(SLOTS)):
        arrived(("a", slot)) if slot != SLOT[0, 0] else None
    if SLOT[0, 0] != 0:
        arrived(("a", 0))
    for made in copies.values():
        made.wait_send()


def local(inputs, weight, cotangent):
    slots = NY * NX
    factor = 1.0 / math.sqrt(slots * NZ * OWN)
    act, dx, gw = pl.pallas_call(
        functools.partial(kernel, factor),
        out_shape=(
            jax.ShapeDtypeStruct((OWN, slots * WIDTH), bf16),
            jax.ShapeDtypeStruct((4, OWN, WIDTH), bf16),
            jax.ShapeDtypeStruct((WIDTH, WIDTH), f32),
        ),
        in_specs=[pl.BlockSpec(memory_space=pltpu.VMEM)] * 3,
        out_specs=[pl.BlockSpec(memory_space=pltpu.VMEM)] * 3,
        scratch_shapes=[
            pltpu.VMEM((slots, NZ, OWN, WIDTH), bf16),
            pltpu.VMEM((slots, NZ, OWN, WIDTH), bf16),
            pltpu.VMEM((slots, OWN, WIDTH), bf16),
            pltpu.VMEM((slots, NZ, OWN, WIDTH), f32),
            pltpu.VMEM((2, 4, slots, OWN, WIDTH), bf16),
            pltpu.VMEM((2, 4, slots, OWN, WIDTH), bf16),
            pltpu.VMEM((slots, OWN, WIDTH), bf16),
            pltpu.VMEM((slots, 4, OWN, WIDTH), bf16),
            pltpu.VMEM((slots, 4, OWN, WIDTH), bf16),
            pltpu.VMEM((NY, 2, 2, 4, OWN, WIDTH), bf16),
            pltpu.VMEM((NY, 2, 2, 4, OWN, WIDTH), bf16),
            pltpu.VMEM((NY, 4, OWN, WIDTH), f32),
            pltpu.VMEM((2, 2, 4, OWN, WIDTH), bf16),
            pltpu.VMEM((2, 2, 4, OWN, WIDTH), bf16),
            pltpu.SemaphoreType.DMA((COPIES,)),
            pltpu.SemaphoreType.DMA((COPIES,)),
            pltpu.SemaphoreType.DMA((3,)),
        ],
        compiler_params=pltpu.CompilerParams(
            collective_id=0, has_side_effects=True, vmem_limit_bytes=56 * 2**20
        ),
        cost_estimate=pl.CostEstimate(flops=7 * 10**9, bytes_accessed=10**7, transcendentals=2 * 10**5),
    )(inputs.reshape(4, OWN, WIDTH), weight[0], cotangent)
    return (act, dx.reshape(4 * OWN, WIDTH), gw[None])


def solution(mesh):
    in_specs = (P(("depth", "col"), "row"), P("col", "row", "depth"), P(("depth", "row"), "col"))
    out_specs = (P(("depth", "row"), "col"), P(("depth", "col"), "row"), P("col", "row", "depth"))
    return jax.shard_map(local, mesh=mesh, in_specs=in_specs, out_specs=out_specs, check_vma=False)
```

```python
import functools
import math

import jax
import jax.numpy as jnp
from jax import lax
from jax.experimental import pallas as pl
from jax.experimental.pallas import tpu as pltpu
from jax.sharding import PartitionSpec as P

MESH = pl.DeviceIdType.MESH
slope_c = math.sqrt(2.0 / math.pi)
bf16, f32 = jnp.bfloat16, jnp.float32
NY, NX, NZ, NC = 4, 4, 8, 2
OWN = 16
WIDTH = 768
HALF = WIDTH // 2
TILE = 256

SLOTS = (
    (2, 2), (3, 2), (0, 2), (1, 3), (3, 3), (2, 1), (2, 3), (1, 2),
    (3, 1), (2, 0), (1, 1), (1, 0), (3, 0), (0, 0), (0, 3), (0, 1),
)
CHUNKS = (
    (0, 1), (1, 1), (2, 3), (5, 3), (8, 1), (9, 2), (11, 2), (13, 1),
    (14, 1), (15, 1),
)
COPIES = 296
FIRST = 7
DIRECT = ()
ORDER = (
    ("s",), ("k", 2), ("k", 3), ("k", 1), ("k", 0), ("m", 7),
    ("r", 7, 0), ("x", 0, 1), ("r", 7, 1), ("x", 0, 3), ("x", 1, 0), ("x", 3, 0),
    ("m", 9), ("r", 9, 0), ("m", 8), ("r", 8, 0), ("r", 7, 2), ("m", 6),
    ("r", 6, 0), ("x", 3, 1), ("r", 9, 1), ("r", 8, 1), ("m", 4), ("r", 4, 0),
    ("x", 3, 3), ("r", 7, 3), ("x", 0, 2), ("r", 6, 1), ("r", 9, 2), ("x", 1, 1),
    ("r", 8, 2), ("r", 4, 1), ("f", 7), ("x", 1, 3), ("r", 6, 2), ("r", 9, 3),
    ("x", 2, 0), ("m", 2), ("x", 3, 2), ("r", 2, 0), ("r", 4, 2), ("x", 1, 2),
    ("m", 5), ("x", 2, 1), ("r", 6, 3), ("m", 1), ("x", 2, 3), ("r", 1, 0),
    ("r", 5, 0), ("r", 2, 1), ("x", 2, 2), ("m", 3), ("r", 4, 3), ("r", 1, 1),
    ("m", 0), ("r", 0, 0), ("r", 3, 0), ("r", 5, 1), ("r", 2, 2), ("r", 1, 2),
    ("r", 0, 1), ("f", 4), ("r", 3, 1), ("r", 2, 3), ("g", 4, 1), ("r", 0, 2),
    ("r", 1, 3), ("r", 3, 2), ("f", 2), ("r", 0, 3), ("f", 1), ("r", 5, 2),
    ("r", 3, 3), ("g", 2, 1), ("g", 1, 1), ("f", 0), ("g", 4, 2), ("f", 3),
    ("g", 2, 2), ("g", 1, 2), ("g", 0, 1), ("r", 5, 3), ("g", 3, 1), ("g", 1, 3),
    ("g", 2, 3), ("g", 0, 2), ("f", 5), ("g", 4, 3), ("f", 6), ("b", 1),
    ("g", 3, 2), ("b", 2), ("d", 1), ("g", 5, 1), ("e", 3), ("b", 4),
    ("g", 0, 3), ("r", 8, 3), ("g", 6, 1), ("d", 2), ("e", 0), ("d", 4),
    ("f", 9), ("g", 3, 3), ("h", 3, 0), ("h", 3, 1), ("g", 5, 2), ("b", 0),
    ("f", 8), ("w", 0, 5, True, False), ("d", 0), ("e", 2), ("g", 9, 1), ("g", 6, 2),
    ("b", 3), ("g", 8, 1), ("g", 5, 3), ("g", 7, 1), ("g", 9, 2), ("d", 3),
    ("e", 1), ("g", 6, 3), ("h", 2, 0), ("g", 8, 2), ("h", 2, 1), ("b", 5),
    ("g", 9, 3), ("g", 7, 2), ("w", 5, 6, False, False), ("d", 5), ("h", 1, 1), ("h", 1, 0),
    ("g", 8, 3), ("b", 6), ("j", 2), ("u",), ("b", 9), ("g", 7, 3),
    ("b", 8), ("d", 6), ("d", 9), ("j", 3), ("h", 0, 0), ("j", 1),
    ("d", 8), ("v", 1), ("v", 0), ("h", 0, 1), ("b", 7), ("w", 11, 5, False, True),
    ("d", 7), ("j", 0), ("z",),
)
SLOT = {name: index for index, name in enumerate(SLOTS)}


def gelu_both(h):
    t = jnp.tanh(slope_c * (h + 0.044715 * h * h * h))
    value = 0.5 * h * (1.0 + t)
    slope = 0.5 * (1.0 + t) + 0.5 * h * (1.0 - t * t) * slope_c * (1.0 + 3.0 * 0.044715 * h * h)
    return value, slope


def kernel(
    factor, x_in, w_in, cot_in, act_out, dx_out, gw_out,
    xs, gh, w, gw, cot, part, ring_out, ring_in, act, swap_out, swap_in, x_out, x_got, total, y_out, y_got, dx,
    send_sem, recv_sem, local_sem,
):
    depth, row, col = lax.axis_index("depth"), lax.axis_index("row"), lax.axis_index("col")
    y, x = depth // NX, lax.rem(depth, NX)

    def at_depth(dy, dx):
        return lax.rem(y + dy, NY) * NX + lax.rem(x + dx, NX)

    def near(dy, dx):
        return (at_depth(dy, dx), row, col)

    def along_z(distance):
        return (depth, lax.rem(row + NZ + distance, NZ), col)

    z_near = (along_z(1), along_z(-1))
    x_near = (near(0, 1), near(0, 3))
    y_near = (near(1, 0), near(3, 0))
    other = (depth, row, 1 - col)
    offsets = [(dy, dx) for dy in range(NY) for dx in range(NX) if (dy, dx) != (0, 0)]

    copies, index_of = {}, {}

    def copy(name, src, dst, device):
        index = len(index_of)
        index_of[name] = index
        made = pltpu.make_async_remote_copy(
            src_ref=src, dst_ref=dst, send_sem=send_sem.at[index], recv_sem=recv_sem.at[index],
            device_id=device, device_id_type=MESH,
        )
        copies[name] = made
        made.start()

    def arrived(name):
        copies[name].wait_recv()

    def each(count, body):
        def step(j, carry):
            body(j)
            return carry
        lax.fori_loop(0, count, step, 0)

    mine = pl.multiple_of(col * 4, 4)
    theirs = pl.multiple_of(4 - col * 4, 4)

    def inputs_to_core(slot):
        block = xs.at[slot, pl.ds(mine, 4)]
        copy(("xc", slot), block, block, other)

    here = pl.ds(pl.multiple_of(depth * WIDTH, WIDTH), WIDTH)
    w_copy = pltpu.make_async_copy(w_in, w, local_sem.at[1])
    cot_copy = pltpu.make_async_copy(cot_in.at[:, here], cot.at[SLOT[0, 0]], local_sem.at[2])
    act_copy = pltpu.make_async_copy(act.at[SLOT[0, 0]], act_out.at[:, here], local_sem.at[3])
    gw_copies = [
        pltpu.make_async_copy(gw.at[pl.ds(j * TILE, TILE)], gw_out.at[pl.ds(j * TILE, TILE)], local_sem.at[4 + j])
        for j in range(WIDTH // TILE)
    ]

    def start():
        barrier = pltpu.get_barrier_semaphore()
        steps = range(1, NZ) if DIRECT else (1, NZ - 1)
        peers = [near(*o) for o in offsets] + [other] + [along_z(step) for step in steps]
        block = xs.at[SLOT[0, 0], pl.ds(mine, 4)]
        own = pltpu.make_async_copy(x_in, block, local_sem.at[0])
        own.start()
        w_copy.start()
        cot_copy.start()
        for peer in peers:
            pl.semaphore_signal(barrier, inc=1, device_id=peer, device_id_type=MESH)
        own.wait()
        pl.semaphore_wait(barrier, len(peers))
        for (dy, dx), device in (((0, 3), x_near[0]), ((0, 1), x_near[1]), ((3, 0), y_near[0]), ((1, 0), y_near[1])):
            copy(("x", dy, dx), block, xs.at[SLOT[dy, dx], pl.ds(mine, 4)], device)
        inputs_to_core(SLOT[0, 0])

    def half_of(slot, half):
        return xs.at[slot, pl.ds(pl.multiple_of(col * 4 + 2 * half, 2), 2)]

    def gather(dy, dx):
        slot = SLOT[dy, dx]
        whole = xs.at[slot, pl.ds(mine, 4)]
        if dx == 2 and dy == 0 or dy == 2:
            arrived(("xh", dy, dx, 0))
            arrived(("xh", dy, dx, 1))
        else:
            arrived(("x", dy, dx))
        if dy == 0:
            if dx == 3:
                copy(("xh", 0, 2, 0), half_of(slot, 0), half_of(SLOT[0, 2], 0), x_near[0])
            if dx == 1:
                copy(("xh", 0, 2, 1), half_of(slot, 1), half_of(SLOT[0, 2], 1), x_near[1])
            copy(("x", 3, dx), whole, xs.at[SLOT[3, dx], pl.ds(mine, 4)], y_near[0])
            copy(("x", 1, dx), whole, xs.at[SLOT[1, dx], pl.ds(mine, 4)], y_near[1])
        if dy == 3:
            copy(("xh", 2, dx, 0), half_of(slot, 0), half_of(SLOT[2, dx], 0), y_near[0])
        if dy == 1:
            copy(("xh", 2, dx, 1), half_of(slot, 1), half_of(SLOT[2, dx], 1), y_near[1])
        inputs_to_core(slot)

    def spread_cot(dy):
        for dx in range(NX):
            if (dy, dx) != (0, 0):
                block = cot_in.at[:, pl.ds(pl.multiple_of(at_depth(dy, dx) * WIDTH, WIDTH), WIDTH)]
                slot = SLOT[(4 - dy) % 4, (4 - dx) % 4]
                copy(("k", slot), block, cot.at[slot], near(dy, dx))

    def forward(c):
        first, count = CHUNKS[c]
        if c == FIRST:
            w_copy.wait()
        for slot in range(first, first + count):
            arrived(("xc", slot))
        block = xs[first : first + count].reshape(count * NZ * OWN, WIDTH)

        def tile(j):
            columns = pl.ds(pl.multiple_of(j * TILE, TILE), TILE)
            terms = jnp.dot(block, w[:, columns], preferred_element_type=f32)
            part[first : first + count, :, :, columns] = terms.reshape(count, NZ, OWN, TILE)

        each(WIDTH // TILE, tile)

    def scatter(c, step):
        first, count = CHUNKS[c]
        slots = pl.ds(first, count)
        for way in range(2):
            owner = lax.rem(row + (4 - step if way == 0 else 4 + step), NZ)
            halves = (slice(0, HALF), slice(HALF, WIDTH))
            if step > 0:
                arrived(("r", c, step - 1, way))

            def add(j):
                s = first + j
                if step == 0:
                    cols = halves[way]
                    ring_out[way, 0, s, :, cols] = part[s, owner, :, cols].astype(bf16)
                elif step == 1:
                    cols, rest = halves[way], halves[1 - way]
                    got = ring_in[way, 0, s, :, cols].astype(f32)
                    ring_out[way, 1, s, :, cols] = (part[s, owner, :, cols] + got).astype(bf16)
                    ring_out[way, 1, s, :, rest] = part[s, owner, :, rest].astype(bf16)
                else:
                    got = ring_in[way, step - 1, s].astype(f32)
                    ring_out[way, step, s] = (part[s, owner] + got).astype(bf16)

            each(count, add)
            cols = halves[way] if step == 0 else slice(0, WIDTH)
            copy(
                ("r", c, step, way), ring_out.at[way, step, slots, :, cols],
                ring_in.at[way, step, slots, :, cols], z_near[way],
            )

    def activate(c):
        first, count = CHUNKS[c]
        arrived(("r", c, 3, 0))
        arrived(("r", c, 3, 1))
        for slot in range(first, first + count):
            if slot != SLOT[0, 0]:
                arrived(("k", slot))
            else:
                cot_copy.wait()

        def one(j):
            s = first + j
            h = part[s, row] + ring_in[0, 3, s].astype(f32) + ring_in[1, 3, s].astype(f32)
            value, slope = gelu_both(h)
            act[s] = value.astype(bf16)
            gh[s, row] = (cot[s].astype(f32) * slope).astype(bf16)

        each(count, one)
        if c in DIRECT:
            spread_direct(c)
        else:
            spread(c, 0)
        for slot in range(first, first + count):
            if slot == SLOT[0, 0]:
                act_copy.start()
            else:
                copy(("a", slot), act.at[slot], act_out.at[:, here], near(*SLOTS[slot]))

    def spread_direct(c):
        first, count = CHUNKS[c]
        for step in range(4):
            for way in range(2):
                cols = slice(0, WIDTH) if step < 3 else (slice(0, HALF), slice(HALF, WIDTH))[way]
                block = gh.at[pl.ds(first, count), row, :, cols]
                copy(("g", c, step, way), block, block, along_z((1 + step) * (1, -1)[way]))

    def spread(c, step):
        first, count = CHUNKS[c]
        slots = pl.ds(first, count)
        for way in range(2):
            if step > 0:
                arrived(("g", c, step - 1, way))
            owner = lax.rem(row + (NZ - step if way == 0 else step), NZ)
            cols = slice(0, WIDTH) if step < 3 else (slice(0, HALF), slice(HALF, WIDTH))[way]
            block = gh.at[slots, owner, :, cols]
            copy(("g", c, step, way), block, block, z_near[way])

    def input_terms(c):
        first, count = CHUNKS[c]
        for step in range(4) if c in DIRECT else (3,):
            arrived(("g", c, step, 0))
            arrived(("g", c, step, 1))
        block = gh[first : first + count].reshape(count * NZ * OWN, WIDTH)

        def tile(j):
            features = pl.ds(pl.multiple_of(j * TILE, TILE), TILE)
            terms = lax.dot_general(
                block, w[features, :], (((1,), (1,)), ((), ())), preferred_element_type=f32
            )
            part[first : first + count, :, :, features] = terms.reshape(count, NZ, OWN, TILE)

        each(WIDTH // TILE, tile)

        def pick(j):
            swap_out[first + j] = part[first + j, pl.ds(theirs, 4)].astype(bf16)

        each(count, pick)
        slots = pl.ds(first, count)
        copy(("d", c), swap_out.at[slots], swap_in.at[slots], other)

    def weight_terms(first, count, is_first, is_last):
        def tile(j):
            features = pl.ds(pl.multiple_of(j * TILE, TILE), TILE)
            tokens = xs[first : first + count, :, :, features].reshape(count * NZ * OWN, TILE)
            grads = gh[first : first + count].reshape(count * NZ * OWN, WIDTH)
            terms = lax.dot_general(
                tokens, grads, (((0,), (0,)), ((), ())), preferred_element_type=f32
            )
            if not is_first:
                terms = terms + gw[features, :]
            if is_last:
                terms = terms * factor
            gw[features, :] = terms

        each(WIDTH // TILE, tile)
        if is_last:
            for made in gw_copies:
                made.start()

    def both(slot, j):
        return part[slot, mine + j] + swap_in[slot, j].astype(f32)

    def swapped(c):
        arrived(("d", c))

    def x_first(dy):
        slot = SLOT[dy, 2]

        def one(j):
            x_out[dy, j // 2, 0, j] = both(slot, j).astype(bf16)

        each(4, one)
        for way in range(2):
            rows = pl.ds(2 * way, 2)
            copy(("e", dy, 0, way), x_out.at[dy, way, 0, rows], x_got.at[dy, way, 0, rows], x_near[way])

    def x_second(dy, way):
        slot = SLOT[dy, (1, 3)[way]]
        arrived(("e", dy, 0, way))

        def with_got(j):
            j = j + 2 * way
            x_out[dy, way, 1, j] = (both(slot, j) + x_got[dy, way, 0, j].astype(f32)).astype(bf16)

        def without(j):
            j = j + 2 * (1 - way)
            x_out[dy, way, 1, j] = both(slot, j).astype(bf16)

        each(2, with_got)
        each(2, without)
        copy(("e", dy, 1, way), x_out.at[dy, way, 1], x_got.at[dy, way, 1], x_near[way])

    def x_last(dy):
        slot = SLOT[dy, 0]
        arrived(("e", dy, 1, 0))
        arrived(("e", dy, 1, 1))

        def one(j):
            total[dy, j] = (
                both(slot, j) + x_got[dy, 0, 1, j].astype(f32) + x_got[dy, 1, 1, j].astype(f32)
            )

        each(4, one)

    def y_first():
        def one(j):
            y_out[j // 2, 0, j] = total[2, j].astype(bf16)

        each(4, one)
        for way in range(2):
            rows = pl.ds(2 * way, 2)
            copy(("y", 0, way), y_out.at[way, 0, rows], y_got.at[way, 0, rows], y_near[way])

    def y_second(way):
        arrived(("y", 0, way))

        def with_got(j):
            j = j + 2 * way
            y_out[way, 1, j] = (total[(1, 3)[way], j] + y_got[way, 0, j].astype(f32)).astype(bf16)

        def without(j):
            j = j + 2 * (1 - way)
            y_out[way, 1, j] = total[(1, 3)[way], j].astype(bf16)

        each(2, with_got)
        each(2, without)
        copy(("y", 1, way), y_out.at[way, 1], y_got.at[way, 1], y_near[way])

    dx_copy = pltpu.make_async_copy(dx, dx_out, local_sem.at[7])

    def y_last():
        arrived(("y", 1, 0))
        arrived(("y", 1, 1))

        def one(j):
            dx[j] = (
                total[0, j] + y_got[0, 1, j].astype(f32) + y_got[1, 1, j].astype(f32)
            ).astype(bf16)

        each(4, one)
        dx_copy.start()

    actions = dict(
        s=start, x=gather, k=spread_cot, m=forward, r=scatter, f=activate, g=spread, b=input_terms,
        w=weight_terms, d=swapped, e=x_first, h=x_second, j=x_last, u=y_first, v=y_second, z=y_last,
    )
    for event in ORDER:
        actions[event[0]](*event[1:])
    for slot in range(len(SLOTS)):
        if slot != SLOT[0, 0]:
            arrived(("a", slot))
    for made in copies.values():
        made.wait_send()
    for made in (dx_copy, act_copy, *gw_copies):
        made.wait()


def hand_over(act, dx, gw, act_out, dx_out, gw_out, act_held, dx_held, gw_held, sem):
    parts = [(gw, gw_held, gw_out, pl.ds(j * 96, 96)) for j in range(WIDTH // 96)]
    parts += [(act, act_held, act_out, pl.ds(0, OWN)), (dx, dx_held, dx_out, pl.ds(0, 4))]
    into = [
        pltpu.make_async_copy(src.at[rows], held.at[rows], sem.at[0, i])
        for i, (src, held, dst, rows) in enumerate(parts)
    ]
    out = [
        pltpu.make_async_copy(held.at[rows], dst.at[rows], sem.at[1, i])
        for i, (src, held, dst, rows) in enumerate(parts)
    ]
    for one in into:
        one.start()
    for one, then in zip(into, out):
        one.wait()
        then.start()
    for one in out:
        one.wait()


def local(inputs, weight, cotangent):
    slots = NY * NX
    factor = 1.0 / math.sqrt(slots * NZ * OWN)
    shapes = (
        jax.ShapeDtypeStruct((OWN, slots * WIDTH), bf16),
        jax.ShapeDtypeStruct((4, OWN, WIDTH), bf16),
        jax.ShapeDtypeStruct((WIDTH, WIDTH), f32),
    )
    anywhere = [pl.BlockSpec(memory_space=pl.ANY)] * 3
    results = pl.pallas_call(
        functools.partial(kernel, factor),
        out_shape=shapes,
        in_specs=anywhere,
        out_specs=anywhere,
        scratch_shapes=[
            pltpu.VMEM((slots, NZ, OWN, WIDTH), bf16),
            pltpu.VMEM((slots, NZ, OWN, WIDTH), bf16),
            pltpu.VMEM((WIDTH, WIDTH), bf16),
            pltpu.VMEM((WIDTH, WIDTH), f32),
            pltpu.VMEM((slots, OWN, WIDTH), bf16),
            pltpu.VMEM((slots, NZ, OWN, WIDTH), f32),
            pltpu.VMEM((2, 4, slots, OWN, WIDTH), bf16),
            pltpu.VMEM((2, 4, slots, OWN, WIDTH), bf16),
            pltpu.VMEM((slots, OWN, WIDTH), bf16),
            pltpu.VMEM((slots, 4, OWN, WIDTH), bf16),
            pltpu.VMEM((slots, 4, OWN, WIDTH), bf16),
            pltpu.VMEM((NY, 2, 2, 4, OWN, WIDTH), bf16),
            pltpu.VMEM((NY, 2, 2, 4, OWN, WIDTH), bf16),
            pltpu.VMEM((NY, 4, OWN, WIDTH), f32),
            pltpu.VMEM((2, 2, 4, OWN, WIDTH), bf16),
            pltpu.VMEM((2, 2, 4, OWN, WIDTH), bf16),
            pltpu.VMEM((4, OWN, WIDTH), bf16),
            pltpu.SemaphoreType.DMA((COPIES,)),
            pltpu.SemaphoreType.DMA((COPIES,)),
            pltpu.SemaphoreType.DMA((8,)),
        ],
        compiler_params=pltpu.CompilerParams(
            collective_id=0, has_side_effects=True, vmem_limit_bytes=56 * 2**20
        ),
        cost_estimate=pl.CostEstimate(flops=7 * 10**9, bytes_accessed=10**7, transcendentals=2 * 10**5),
    )(inputs.reshape(4, OWN, WIDTH), weight[0], cotangent)
    act, dx, gw = pl.pallas_call(
        hand_over,
        out_shape=shapes,
        in_specs=anywhere,
        out_specs=anywhere,
        scratch_shapes=[pltpu.VMEM(one.shape, one.dtype) for one in shapes]
        + [pltpu.SemaphoreType.DMA((2, 2 + WIDTH // 96))],
    )(*results)
    return (act, dx.reshape(4 * OWN, WIDTH), gw[None])


def solution(mesh):
    in_specs = (P(("depth", "col"), "row"), P("col", "row", "depth"), P(("depth", "row"), "col"))
    out_specs = (P(("depth", "row"), "col"), P(("depth", "col"), "row"), P("col", "row", "depth"))
    return jax.shard_map(local, mesh=mesh, in_specs=in_specs, out_specs=out_specs, check_vma=False)
```

```python
import functools
import math

import jax
import jax.numpy as jnp
from jax import lax
from jax.experimental import pallas as pl
from jax.experimental.pallas import tpu as pltpu
from jax.sharding import PartitionSpec as P

MESH = pl.DeviceIdType.MESH
slope_c = math.sqrt(2.0 / math.pi)
bf16, f32 = jnp.bfloat16, jnp.float32
NY, NX, NZ, NC = 4, 4, 8, 2
OWN = 16
WIDTH = 768
HALF = WIDTH // 2
TILE = 256

SLOTS = (
    (1, 1), (2, 2), (3, 2), (2, 3), (2, 1), (3, 3), (1, 2), (1, 3),
    (2, 0), (3, 1), (0, 2), (0, 1), (1, 0), (3, 0), (0, 3), (0, 0),
)
CHUNKS = (
    (0, 2), (2, 1), (3, 2), (5, 1), (6, 2), (8, 1), (9, 2), (11, 2),
    (13, 2), (15, 1),
)
COPIES = 296
FIRST = 9
DIRECT = ()
ORDER = (
    ("s",), ("m", 9), ("r", 9, 0), ("x", 0, 3), ("x", 3, 0), ("x", 1, 0),
    ("x", 0, 1), ("r", 9, 1), ("m", 8), ("r", 8, 0), ("m", 7), ("x", 3, 3),
    ("r", 7, 0), ("x", 1, 3), ("r", 9, 2), ("x", 2, 0), ("x", 0, 2), ("m", 3),
    ("r", 3, 0), ("r", 8, 1), ("x", 3, 1), ("m", 5), ("r", 5, 0), ("r", 7, 1),
    ("r", 9, 3), ("m", 6), ("r", 6, 0), ("x", 3, 2), ("x", 1, 1), ("x", 2, 3),
    ("r", 3, 1), ("x", 1, 2), ("r", 8, 2), ("k", 2), ("r", 5, 1), ("r", 7, 2),
    ("m", 1), ("r", 1, 0), ("r", 6, 1), ("x", 2, 2), ("r", 3, 2), ("r", 8, 3),
    ("x", 2, 1), ("m", 0), ("r", 0, 0), ("r", 7, 3), ("m", 2), ("r", 1, 1),
    ("m", 4), ("r", 2, 0), ("r", 4, 0), ("r", 5, 2), ("r", 0, 1), ("k", 0),
    ("r", 6, 2), ("r", 1, 2), ("r", 2, 1), ("k", 1), ("r", 4, 1), ("r", 3, 3),
    ("r", 0, 2), ("r", 5, 3), ("r", 1, 3), ("r", 6, 3), ("r", 2, 2), ("r", 0, 3),
    ("r", 4, 2), ("k", 3), ("f", 6), ("r", 2, 3), ("f", 3), ("f", 1),
    ("f", 0), ("r", 4, 3), ("f", 2), ("g", 1, 1), ("f", 5), ("g", 0, 1),
    ("f", 4), ("g", 2, 1), ("g", 1, 2), ("g", 3, 1), ("g", 0, 2), ("g", 4, 1),
    ("g", 5, 1), ("f", 9), ("g", 2, 2), ("g", 0, 3), ("g", 1, 3), ("g", 4, 2),
    ("g", 6, 1), ("g", 2, 3), ("f", 7), ("f", 8), ("g", 5, 2), ("b", 0),
    ("g", 4, 3), ("g", 3, 2), ("b", 1), ("g", 6, 2), ("b", 2), ("g", 7, 1),
    ("d", 0), ("w", 0, 5, 1, 0), ("e", 2), ("g", 8, 1), ("g", 5, 3), ("g", 9, 1),
    ("d", 1), ("b", 4), ("d", 2), ("e", 3), ("g", 6, 3), ("g", 3, 3),
    ("g", 7, 2), ("d", 4), ("e", 1), ("h", 2, 0), ("g", 8, 2), ("h", 2, 1),
    ("b", 5), ("g", 9, 2), ("b", 6), ("h", 1, 0), ("g", 7, 3), ("d", 5),
    ("b", 3), ("g", 8, 3), ("d", 6), ("h", 3, 0), ("h", 1, 1), ("g", 9, 3),
    ("j", 2), ("e", 0), ("d", 3), ("h", 3, 1), ("u",), ("b", 7),
    ("b", 8), ("b", 9), ("d", 7), ("j", 1), ("v", 0), ("h", 0, 0),
    ("d", 8), ("h", 0, 1), ("j", 3), ("v", 1), ("w", 5, 6, 0, 0), ("w", 11, 5, 0, 1),
    ("d", 9), ("j", 0), ("z",),
)
SLOT = {name: index for index, name in enumerate(SLOTS)}


def gelu_both(h):
    t = jnp.tanh(slope_c * (h + 0.044715 * h * h * h))
    value = 0.5 * h * (1.0 + t)
    slope = 0.5 * (1.0 + t) + 0.5 * h * (1.0 - t * t) * slope_c * (1.0 + 3.0 * 0.044715 * h * h)
    return value, slope


def kernel(
    factor, x_in, w_in, cot_in, act_out, dx, gw,
    xs, gh, w, cot, part, ring_out, ring_in, act, swap_out, swap_in, x_out, x_got, total, y_out, y_got,
    send_sem, recv_sem, local_sem,
):
    depth, row, col = lax.axis_index("depth"), lax.axis_index("row"), lax.axis_index("col")
    y, x = depth // NX, lax.rem(depth, NX)

    def at_depth(dy, dx):
        return lax.rem(y + dy, NY) * NX + lax.rem(x + dx, NX)

    def near(dy, dx):
        return (at_depth(dy, dx), row, col)

    def along_z(distance):
        return (depth, lax.rem(row + NZ + distance, NZ), col)

    z_near = (along_z(1), along_z(-1))
    first_near = (near(col, 1 - col), near(3 * col, 3 - 3 * col))
    second_near = (near(1 - col, col), near(3 - 3 * col, 3 * col))

    def slot_at(second, first):
        there, turned = SLOT[second, first], SLOT[first, second]
        return there if there == turned else there + col * (turned - there)

    other = (depth, row, 1 - col)
    offsets = [(dy, dx) for dy in range(NY) for dx in range(NX) if (dy, dx) != (0, 0)]

    copies, index_of = {}, {}

    def copy(name, src, dst, device):
        index = len(index_of)
        index_of[name] = index
        made = pltpu.make_async_remote_copy(
            src_ref=src, dst_ref=dst, send_sem=send_sem.at[index], recv_sem=recv_sem.at[index],
            device_id=device, device_id_type=MESH,
        )
        copies[name] = made
        made.start()

    waited = set()

    def arrived(name):
        if name not in waited:
            copies[name].wait_recv()
            waited.add(name)

    def each(count, body):
        def step(j, carry):
            body(j)
            return carry
        lax.fori_loop(0, count, step, 0)

    mine = pl.multiple_of(col * 4, 4)
    theirs = pl.multiple_of(4 - col * 4, 4)

    def inputs_to_core(second, first):
        block = xs.at[slot_at(second, first), pl.ds(mine, 4)]
        copy(("xc", second, first), block, block, other)

    here = pl.ds(pl.multiple_of(depth * WIDTH, WIDTH), WIDTH)
    w_copy = pltpu.make_async_copy(w_in, w, local_sem.at[1])
    cot_copy = pltpu.make_async_copy(cot_in.at[:, here], cot.at[SLOT[0, 0]], local_sem.at[2])
    act_copy = pltpu.make_async_copy(act.at[SLOT[0, 0]], act_out.at[:, here], local_sem.at[3])

    def start():
        barrier = pltpu.get_barrier_semaphore()
        steps = range(1, NZ) if DIRECT else (1, NZ - 1)
        peers = [near(*o) for o in offsets] + [other] + [along_z(step) for step in steps]
        block = xs.at[SLOT[0, 0], pl.ds(mine, 4)]
        own = pltpu.make_async_copy(x_in, block, local_sem.at[0])
        own.start()
        w_copy.start()
        cot_copy.start()
        for peer in peers:
            pl.semaphore_signal(barrier, inc=1, device_id=peer, device_id_type=MESH)
        own.wait()
        pl.semaphore_wait(barrier, len(peers))
        for (dy, dx), device in (((0, 3), first_near[0]), ((0, 1), first_near[1]), ((3, 0), second_near[0]), ((1, 0), second_near[1])):
            copy(("x", dy, dx), block, xs.at[slot_at(dy, dx), pl.ds(mine, 4)], device)
        inputs_to_core(0, 0)

    def half_of(slot, half):
        return xs.at[slot, pl.ds(pl.multiple_of(col * 4 + 2 * half, 2), 2)]

    def gather(second, first):
        slot = slot_at(second, first)
        whole = xs.at[slot, pl.ds(mine, 4)]
        if first == 2 and second == 0 or second == 2:
            arrived(("xh", second, first, 0))
            arrived(("xh", second, first, 1))
        else:
            arrived(("x", second, first))
        if second == 0:
            if first == 3:
                copy(("xh", 0, 2, 0), half_of(slot, 0), half_of(slot_at(0, 2), 0), first_near[0])
            if first == 1:
                copy(("xh", 0, 2, 1), half_of(slot, 1), half_of(slot_at(0, 2), 1), first_near[1])
            copy(("x", 3, first), whole, xs.at[slot_at(3, first), pl.ds(mine, 4)], second_near[0])
            copy(("x", 1, first), whole, xs.at[slot_at(1, first), pl.ds(mine, 4)], second_near[1])
        if second == 3:
            copy(("xh", 2, first, 0), half_of(slot, 0), half_of(slot_at(2, first), 0), second_near[0])
        if second == 1:
            copy(("xh", 2, first, 1), half_of(slot, 1), half_of(slot_at(2, first), 1), second_near[1])
        inputs_to_core(second, first)

    def spread_cot(dy):
        for dx in range(NX):
            if (dy, dx) != (0, 0):
                block = cot_in.at[:, pl.ds(pl.multiple_of(at_depth(dy, dx) * WIDTH, WIDTH), WIDTH)]
                slot = SLOT[(4 - dy) % 4, (4 - dx) % 4]
                copy(("k", slot), block, cot.at[slot], near(dy, dx))

    def forward(c):
        first, count = CHUNKS[c]
        if c == FIRST:
            w_copy.wait()
        for slot in range(first, first + count):
            dy, dx = SLOTS[slot]
            arrived(("xc", dy, dx))
            arrived(("xc", dx, dy))
        block = xs[first : first + count].reshape(count * NZ * OWN, WIDTH)

        def tile(j):
            columns = pl.ds(pl.multiple_of(j * TILE, TILE), TILE)
            terms = jnp.dot(block, w[:, columns], preferred_element_type=f32)
            part[first : first + count, :, :, columns] = terms.reshape(count, NZ, OWN, TILE)

        each(WIDTH // TILE, tile)

    def scatter(c, step):
        first, count = CHUNKS[c]
        slots = pl.ds(first, count)
        for way in range(2):
            owner = lax.rem(row + (4 - step if way == 0 else 4 + step), NZ)
            halves = (slice(0, HALF), slice(HALF, WIDTH))
            if step > 0:
                arrived(("r", c, step - 1, way))

            def add(j):
                s = first + j
                if step == 0:
                    cols = halves[way]
                    ring_out[way, 0, s, :, cols] = part[s, owner, :, cols].astype(bf16)
                elif step == 1:
                    cols, rest = halves[way], halves[1 - way]
                    got = ring_in[way, 0, s, :, cols].astype(f32)
                    ring_out[way, 1, s, :, cols] = (part[s, owner, :, cols] + got).astype(bf16)
                    ring_out[way, 1, s, :, rest] = part[s, owner, :, rest].astype(bf16)
                else:
                    got = ring_in[way, step - 1, s].astype(f32)
                    ring_out[way, step, s] = (part[s, owner] + got).astype(bf16)

            each(count, add)
            cols = halves[way] if step == 0 else slice(0, WIDTH)
            copy(
                ("r", c, step, way), ring_out.at[way, step, slots, :, cols],
                ring_in.at[way, step, slots, :, cols], z_near[way],
            )

    def activate(c):
        first, count = CHUNKS[c]
        arrived(("r", c, 3, 0))
        arrived(("r", c, 3, 1))
        for slot in range(first, first + count):
            if slot != SLOT[0, 0]:
                arrived(("k", slot))
            else:
                cot_copy.wait()

        def one(j):
            s = first + j
            h = part[s, row] + ring_in[0, 3, s].astype(f32) + ring_in[1, 3, s].astype(f32)
            value, slope = gelu_both(h)
            act[s] = value.astype(bf16)
            gh[s, row] = (cot[s].astype(f32) * slope).astype(bf16)

        each(count, one)
        if c in DIRECT:
            spread_direct(c)
        else:
            spread(c, 0)
        for slot in range(first, first + count):
            if slot == SLOT[0, 0]:
                act_copy.start()
            else:
                copy(("a", slot), act.at[slot], act_out.at[:, here], near(*SLOTS[slot]))

    def spread_direct(c):
        first, count = CHUNKS[c]
        for step in range(4):
            for way in range(2):
                cols = slice(0, WIDTH) if step < 3 else (slice(0, HALF), slice(HALF, WIDTH))[way]
                block = gh.at[pl.ds(first, count), row, :, cols]
                copy(("g", c, step, way), block, block, along_z((1 + step) * (1, -1)[way]))

    def spread(c, step):
        first, count = CHUNKS[c]
        slots = pl.ds(first, count)
        for way in range(2):
            if step > 0:
                arrived(("g", c, step - 1, way))
            owner = lax.rem(row + (NZ - step if way == 0 else step), NZ)
            cols = slice(0, WIDTH) if step < 3 else (slice(0, HALF), slice(HALF, WIDTH))[way]
            block = gh.at[slots, owner, :, cols]
            copy(("g", c, step, way), block, block, z_near[way])

    def input_terms(c):
        first, count = CHUNKS[c]
        for step in range(4) if c in DIRECT else (3,):
            arrived(("g", c, step, 0))
            arrived(("g", c, step, 1))
        block = gh[first : first + count].reshape(count * NZ * OWN, WIDTH)

        def tile(j):
            features = pl.ds(pl.multiple_of(j * TILE, TILE), TILE)
            terms = lax.dot_general(
                block, w[features, :], (((1,), (1,)), ((), ())), preferred_element_type=f32
            )
            part[first : first + count, :, :, features] = terms.reshape(count, NZ, OWN, TILE)

        each(WIDTH // TILE, tile)

        def pick(j):
            swap_out[first + j] = part[first + j, pl.ds(theirs, 4)].astype(bf16)

        each(count, pick)
        slots = pl.ds(first, count)
        copy(("d", c), swap_out.at[slots], swap_in.at[slots], other)

    def weight_terms(first, count, is_first, is_last):
        def tile(j):
            features = pl.ds(pl.multiple_of(j * TILE, TILE), TILE)
            tokens = xs[first : first + count, :, :, features].reshape(count * NZ * OWN, TILE)
            grads = gh[first : first + count].reshape(count * NZ * OWN, WIDTH)
            terms = lax.dot_general(
                tokens, grads, (((0,), (0,)), ((), ())), preferred_element_type=f32
            )
            if not is_first:
                terms = terms + gw[features, :]
            if is_last:
                terms = terms * factor
            gw[features, :] = terms

        each(WIDTH // TILE, tile)

    def both(slot, j):
        return part[slot, mine + j] + swap_in[slot, j].astype(f32)

    def swapped(c):
        arrived(("d", c))

    def x_first(dy):
        slot = slot_at(dy, 2)

        def one(j):
            x_out[dy, j // 2, 0, j] = both(slot, j).astype(bf16)

        each(4, one)
        for way in range(2):
            rows = pl.ds(2 * way, 2)
            copy(("e", dy, 0, way), x_out.at[dy, way, 0, rows], x_got.at[dy, way, 0, rows], first_near[way])

    def x_second(dy, way):
        slot = slot_at(dy, (1, 3)[way])
        arrived(("e", dy, 0, way))

        def with_got(j):
            j = j + 2 * way
            x_out[dy, way, 1, j] = (both(slot, j) + x_got[dy, way, 0, j].astype(f32)).astype(bf16)

        def without(j):
            j = j + 2 * (1 - way)
            x_out[dy, way, 1, j] = both(slot, j).astype(bf16)

        each(2, with_got)
        each(2, without)
        copy(("e", dy, 1, way), x_out.at[dy, way, 1], x_got.at[dy, way, 1], first_near[way])

    def x_last(dy):
        slot = slot_at(dy, 0)
        arrived(("e", dy, 1, 0))
        arrived(("e", dy, 1, 1))

        def one(j):
            total[dy, j] = (
                both(slot, j) + x_got[dy, 0, 1, j].astype(f32) + x_got[dy, 1, 1, j].astype(f32)
            )

        each(4, one)

    def y_first():
        def one(j):
            y_out[j // 2, 0, j] = total[2, j].astype(bf16)

        each(4, one)
        for way in range(2):
            rows = pl.ds(2 * way, 2)
            copy(("y", 0, way), y_out.at[way, 0, rows], y_got.at[way, 0, rows], second_near[way])

    def y_second(way):
        arrived(("y", 0, way))

        def with_got(j):
            j = j + 2 * way
            y_out[way, 1, j] = (total[(1, 3)[way], j] + y_got[way, 0, j].astype(f32)).astype(bf16)

        def without(j):
            j = j + 2 * (1 - way)
            y_out[way, 1, j] = total[(1, 3)[way], j].astype(bf16)

        each(2, with_got)
        each(2, without)
        copy(("y", 1, way), y_out.at[way, 1], y_got.at[way, 1], second_near[way])

    def y_last():
        arrived(("y", 1, 0))
        arrived(("y", 1, 1))

        def one(j):
            dx[j] = (
                total[0, j] + y_got[0, 1, j].astype(f32) + y_got[1, 1, j].astype(f32)
            ).astype(bf16)

        each(4, one)

    actions = dict(
        s=start, x=gather, k=spread_cot, m=forward, r=scatter, f=activate, g=spread, b=input_terms,
        w=weight_terms, d=swapped, e=x_first, h=x_second, j=x_last, u=y_first, v=y_second, z=y_last,
    )
    for event in ORDER:
        actions[event[0]](*event[1:])
    for slot in range(len(SLOTS)):
        if slot != SLOT[0, 0]:
            arrived(("a", slot))
    for made in copies.values():
        made.wait_send()
    act_copy.wait()


def local(inputs, weight, cotangent):
    slots = NY * NX
    factor = 1.0 / math.sqrt(slots * NZ * OWN)
    shapes = (
        pltpu.VMEM((OWN, slots * WIDTH), bf16),
        pltpu.VMEM((4, OWN, WIDTH), bf16),
        pltpu.VMEM((WIDTH, WIDTH), f32),
    )
    anywhere = [pl.BlockSpec(memory_space=pl.ANY)] * 3
    act, dx, gw = pl.pallas_call(
        functools.partial(kernel, factor),
        out_shape=shapes,
        in_specs=anywhere,
        out_specs=[pl.BlockSpec(memory_space=pltpu.VMEM)] * 3,
        scratch_shapes=[
            pltpu.VMEM((slots, NZ, OWN, WIDTH), bf16),
            pltpu.VMEM((slots, NZ, OWN, WIDTH), bf16),
            pltpu.VMEM((WIDTH, WIDTH), bf16),
            pltpu.VMEM((slots, OWN, WIDTH), bf16),
            pltpu.VMEM((slots, NZ, OWN, WIDTH), f32),
            pltpu.VMEM((2, 4, slots, OWN, WIDTH), bf16),
            pltpu.VMEM((2, 4, slots, OWN, WIDTH), bf16),
            pltpu.VMEM((slots, OWN, WIDTH), bf16),
            pltpu.VMEM((slots, 4, OWN, WIDTH), bf16),
            pltpu.VMEM((slots, 4, OWN, WIDTH), bf16),
            pltpu.VMEM((NY, 2, 2, 4, OWN, WIDTH), bf16),
            pltpu.VMEM((NY, 2, 2, 4, OWN, WIDTH), bf16),
            pltpu.VMEM((NY, 4, OWN, WIDTH), f32),
            pltpu.VMEM((2, 2, 4, OWN, WIDTH), bf16),
            pltpu.VMEM((2, 2, 4, OWN, WIDTH), bf16),
            pltpu.SemaphoreType.DMA((COPIES,)),
            pltpu.SemaphoreType.DMA((COPIES,)),
            pltpu.SemaphoreType.DMA((4,)),
        ],
        compiler_params=pltpu.CompilerParams(
            collective_id=0, has_side_effects=True, vmem_limit_bytes=56 * 2**20
        ),
        cost_estimate=pl.CostEstimate(flops=7 * 10**9, bytes_accessed=10**7, transcendentals=2 * 10**5),
    )(inputs.reshape(4, OWN, WIDTH), weight[0], cotangent)
    return (act, dx.reshape(4 * OWN, WIDTH), gw[None])


def solution(mesh):
    in_specs = (P(("depth", "col"), "row"), P("col", "row", "depth"), P(("depth", "row"), "col"))
    out_specs = (P(("depth", "row"), "col"), P(("depth", "col"), "row"), P("col", "row", "depth"))
    return jax.shard_map(local, mesh=mesh, in_specs=in_specs, out_specs=out_specs, check_vma=False)
```

```python
import functools
import math

import jax
import jax.numpy as jnp
from jax import lax
from jax.experimental import pallas as pl
from jax.experimental.pallas import tpu as pltpu
from jax.sharding import PartitionSpec as P

MESH = pl.DeviceIdType.MESH
slope_c = math.sqrt(2.0 / math.pi)
bf16, f32 = jnp.bfloat16, jnp.float32
NY, NX, NZ, NC = 4, 4, 8, 2
OWN = 16
WIDTH = 768
HALF = WIDTH // 2
TILE = 256
SEND_LAG = 24

SLOTS = (
    (3, 2), (1, 1), (3, 3), (2, 2), (2, 3), (1, 2), (2, 1), (1, 3),
    (2, 0), (3, 1), (0, 2), (0, 1), (1, 0), (3, 0), (0, 3), (0, 0),
)
CHUNKS = (
    (0, 2), (2, 1), (3, 1), (4, 3), (7, 1), (8, 1), (9, 2), (11, 2),
    (13, 2), (15, 1),
)
COPIES = 296
FIRST = 9
ORDER = (
    ("s",), ("m", 9), ("r", 9, 0), ("x", 0, 3), ("x", 3, 0), ("x", 1, 0),
    ("x", 0, 1), ("r", 9, 1), ("m", 8), ("r", 8, 0), ("m", 7), ("x", 3, 3),
    ("x", 1, 3), ("r", 7, 0), ("x", 2, 0), ("k", 3, 3), ("x", 0, 2), ("r", 9, 2),
    ("m", 1), ("x", 3, 1), ("r", 1, 0), ("x", 1, 1), ("r", 8, 1), ("m", 5),
    ("r", 5, 0), ("r", 7, 1), ("m", 6), ("r", 6, 0), ("x", 3, 2), ("r", 9, 3),
    ("x", 2, 3), ("r", 1, 1), ("m", 4), ("r", 4, 0), ("x", 2, 1), ("r", 8, 2),
    ("x", 1, 2), ("r", 5, 1), ("k", 0, 2), ("k", 3, 2), ("m", 0), ("r", 0, 0),
    ("r", 6, 1), ("m", 3), ("r", 3, 0), ("k", 0, 3), ("r", 4, 1), ("x", 2, 2),
    ("r", 1, 2), ("k", 2, 0), ("k", 3, 1), ("r", 7, 2), ("k", 2, 3), ("k", 2, 2),
    ("k", 1, 2), ("m", 2), ("r", 2, 0), ("r", 0, 1), ("r", 6, 2), ("r", 3, 1),
    ("r", 4, 2), ("r", 2, 1), ("r", 5, 2), ("k", 2, 1), ("r", 6, 3), ("k", 1, 3),
    ("r", 0, 2), ("r", 4, 3), ("k", 3, 0), ("r", 3, 2), ("r", 2, 2), ("f", 6),
    ("k", 0, 1), ("r", 5, 3), ("r", 7, 3), ("r", 0, 3), ("r", 2, 3), ("k", 1, 1),
    ("r", 3, 3), ("f", 4), ("f", 7), ("f", 0), ("r", 8, 3), ("k", 1, 0),
    ("f", 2), ("f", 3), ("g", 4, 1), ("f", 5), ("g", 0, 1), ("r", 1, 3),
    ("g", 2, 1), ("g", 3, 1), ("g", 6, 1), ("g", 5, 1), ("g", 2, 2), ("g", 0, 2),
    ("g", 3, 2), ("f", 1), ("g", 2, 3), ("g", 4, 2), ("f", 8), ("g", 5, 2),
    ("g", 3, 3), ("g", 0, 3), ("g", 1, 1), ("g", 6, 2), ("b", 2, 1), ("g", 7, 1),
    ("g", 8, 1), ("d", 2), ("f", 9), ("e", 2), ("b", 3, 1), ("g", 1, 2),
    ("g", 4, 3), ("g", 5, 3), ("b", 0, 1), ("g", 6, 3), ("g", 7, 2), ("w", 0, 2, 1, 0),
    ("g", 8, 2), ("d", 3), ("e", 1), ("d", 0), ("h", 2, 1), ("g", 1, 3),
    ("g", 9, 1), ("e", 3), ("h", 2, 0), ("b", 4, 3), ("g", 7, 3), ("h", 1, 0),
    ("g", 8, 3), ("b", 1, 1), ("g", 9, 2), ("d", 4), ("h", 1, 1), ("j", 2),
    ("e", 0), ("u",), ("h", 3, 0), ("d", 1), ("h", 3, 1), ("b", 7, 1),
    ("b", 8, 1), ("g", 9, 3), ("d", 7), ("d", 8), ("h", 0, 1), ("h", 0, 0),
    ("j", 1), ("v", 0), ("j", 3), ("v", 1), ("b", 9, 1), ("w", 2, 14, 0, 1),
    ("d", 9), ("j", 0), ("z",),
)
SLOT = {name: index for index, name in enumerate(SLOTS)}


def gelu_both(h):
    t = jnp.tanh(slope_c * (h + 0.044715 * h * h * h))
    value = 0.5 * h * (1.0 + t)
    slope = 0.5 * (1.0 + t) + 0.5 * h * (1.0 - t * t) * slope_c * (1.0 + 3.0 * 0.044715 * h * h)
    return value, slope


def kernel(
    factor, x_in, w_in, cot_in, act_out, dx, gw,
    xs, gh, w, cot, part, ring_out, ring_in, act, swap_in, x_out, x_got, total, y_out, y_got,
    send_sem, recv_sem, local_sem,
):
    depth, row, col = lax.axis_index("depth"), lax.axis_index("row"), lax.axis_index("col")
    y, x = depth // NX, lax.rem(depth, NX)

    def at_depth(dy, dx):
        return lax.rem(y + dy, NY) * NX + lax.rem(x + dx, NX)

    def near(dy, dx):
        return (at_depth(dy, dx), row, col)

    def along_z(distance):
        return (depth, lax.rem(row + NZ + distance, NZ), col)

    z_near = (along_z(1), along_z(-1))
    first_near = (near(col, 1 - col), near(3 * col, 3 - 3 * col))
    second_near = (near(1 - col, col), near(3 - 3 * col, 3 * col))

    def slot_at(second, first):
        there, turned = SLOT[second, first], SLOT[first, second]
        return there if there == turned else there + col * (turned - there)

    other = (depth, row, 1 - col)
    copies, index_of = {}, {}

    def copy(name, src, dst, device):
        index = len(index_of)
        index_of[name] = index
        made = pltpu.make_async_remote_copy(
            src_ref=src, dst_ref=dst, send_sem=send_sem.at[index], recv_sem=recv_sem.at[index],
            device_id=device, device_id_type=MESH,
        )
        copies[name] = made
        made.start()

    waited = set()

    def arrived(name):
        if name not in waited:
            copies[name].wait_recv()
            waited.add(name)

    def each(count, body):
        def step(j, carry):
            body(j)
            return carry
        lax.fori_loop(0, count, step, 0)

    mine = pl.multiple_of(col * 4, 4)
    theirs = pl.multiple_of(4 - col * 4, 4)

    def inputs_to_core(second, first):
        block = xs.at[slot_at(second, first), pl.ds(mine, 4)]
        copy(("xc", second, first), block, block, other)

    here = pl.ds(pl.multiple_of(depth * WIDTH, WIDTH), WIDTH)
    w_copy = pltpu.make_async_copy(w_in, w, local_sem.at[1])
    cot_copy = pltpu.make_async_copy(cot_in.at[:, here], cot.at[SLOT[0, 0]], local_sem.at[2])
    act_copy = pltpu.make_async_copy(act.at[SLOT[0, 0]], act_out.at[:, here], local_sem.at[3])

    def start():
        barrier = pltpu.get_barrier_semaphore()
        peers = [*first_near, *second_near, other, *z_near]
        block = xs.at[SLOT[0, 0], pl.ds(mine, 4)]
        own = pltpu.make_async_copy(x_in, block, local_sem.at[0])
        own.start()
        w_copy.start()
        cot_copy.start()
        for peer in peers:
            pl.semaphore_signal(barrier, inc=1, device_id=peer, device_id_type=MESH)
        own.wait()
        pl.semaphore_wait(barrier, len(peers))
        for (dy, dx), device in (((0, 3), first_near[0]), ((0, 1), first_near[1]), ((3, 0), second_near[0]), ((1, 0), second_near[1])):
            copy(("x", dy, dx), block, xs.at[slot_at(dy, dx), pl.ds(mine, 4)], device)
        inputs_to_core(0, 0)

    def half_of(slot, half):
        return xs.at[slot, pl.ds(pl.multiple_of(col * 4 + 2 * half, 2), 2)]

    def gather(second, first):
        slot = slot_at(second, first)
        whole = xs.at[slot, pl.ds(mine, 4)]
        if first == 2 and second == 0 or second == 2:
            arrived(("xh", second, first, 0))
            arrived(("xh", second, first, 1))
        else:
            arrived(("x", second, first))
        if second == 0:
            if first == 3:
                copy(("xh", 0, 2, 0), half_of(slot, 0), half_of(slot_at(0, 2), 0), first_near[0])
            if first == 1:
                copy(("xh", 0, 2, 1), half_of(slot, 1), half_of(slot_at(0, 2), 1), first_near[1])
            copy(("x", 3, first), whole, xs.at[slot_at(3, first), pl.ds(mine, 4)], second_near[0])
            copy(("x", 1, first), whole, xs.at[slot_at(1, first), pl.ds(mine, 4)], second_near[1])
        if second == 3:
            copy(("xh", 2, first, 0), half_of(slot, 0), half_of(slot_at(2, first), 0), second_near[0])
        if second == 1:
            copy(("xh", 2, first, 1), half_of(slot, 1), half_of(slot_at(2, first), 1), second_near[1])
        inputs_to_core(second, first)

    def spread_cot(dy, dx):
        block = cot_in.at[:, pl.ds(pl.multiple_of(at_depth(dy, dx) * WIDTH, WIDTH), WIDTH)]
        slot = SLOT[(4 - dy) % 4, (4 - dx) % 4]
        copy(("k", slot), block, cot.at[slot], near(dy, dx))

    def forward(c):
        first, count = CHUNKS[c]
        if c == FIRST:
            w_copy.wait()
        for slot in range(first, first + count):
            dy, dx = SLOTS[slot]
            arrived(("xc", dy, dx))
            arrived(("xc", dx, dy))
        block = xs[first : first + count].reshape(count * NZ * OWN, WIDTH)

        def tile(j):
            columns = pl.ds(pl.multiple_of(j * TILE, TILE), TILE)
            terms = jnp.dot(block, w[:, columns], preferred_element_type=f32)
            part[first : first + count, :, :, columns] = terms.reshape(count, NZ, OWN, TILE)

        each(WIDTH // TILE, tile)

    def scatter(c, step):
        first, count = CHUNKS[c]
        slots = pl.ds(first, count)
        for way in range(2):
            owner = lax.rem(row + (4 - step if way == 0 else 4 + step), NZ)
            halves = (slice(0, HALF), slice(HALF, WIDTH))
            if step > 0:
                arrived(("r", c, step - 1, way))

            def add(j):
                s = first + j
                if step == 0:
                    cols = halves[way]
                    ring_out[way, 0, s, :, cols] = part[s, owner, :, cols].astype(bf16)
                elif step == 1:
                    cols, rest = halves[way], halves[1 - way]
                    got = ring_in[way, 0, s, :, cols].astype(f32)
                    ring_out[way, 1, s, :, cols] = (part[s, owner, :, cols] + got).astype(bf16)
                    ring_out[way, 1, s, :, rest] = part[s, owner, :, rest].astype(bf16)
                else:
                    got = ring_in[way, step - 1, s].astype(f32)
                    ring_out[way, step, s] = (part[s, owner] + got).astype(bf16)

            each(count, add)
            cols = halves[way] if step == 0 else slice(0, WIDTH)
            copy(
                ("r", c, step, way), ring_out.at[way, step, slots, :, cols],
                ring_in.at[way, step, slots, :, cols], z_near[way],
            )

    def activate(c):
        first, count = CHUNKS[c]
        arrived(("r", c, 3, 0))
        arrived(("r", c, 3, 1))
        for slot in range(first, first + count):
            if slot != SLOT[0, 0]:
                arrived(("k", slot))
            else:
                cot_copy.wait()

        def one(j):
            s = first + j
            h = part[s, row] + ring_in[0, 3, s].astype(f32) + ring_in[1, 3, s].astype(f32)
            value, slope = gelu_both(h)
            act[s] = value.astype(bf16)
            gh[s, row] = (cot[s].astype(f32) * slope).astype(bf16)

        each(count, one)
        spread(c, 0)
        for slot in range(first, first + count):
            if slot == SLOT[0, 0]:
                act_copy.start()
            else:
                copy(("a", slot), act.at[slot], act_out.at[:, here], near(*SLOTS[slot]))

    def spread(c, step):
        first, count = CHUNKS[c]
        slots = pl.ds(first, count)
        for way in range(2):
            if step > 0:
                arrived(("g", c, step - 1, way))
            owner = lax.rem(row + (NZ - step if way == 0 else step), NZ)
            cols = slice(0, WIDTH) if step < 3 else (slice(0, HALF), slice(HALF, WIDTH))[way]
            block = gh.at[slots, owner, :, cols]
            copy(("g", c, step, way), block, block, z_near[way])

    def input_terms(c, chunks):
        first, count = CHUNKS[c][0], sum(CHUNKS[c + i][1] for i in range(chunks))
        for i in range(c, c + chunks):
            arrived(("g", i, 3, 0))
            arrived(("g", i, 3, 1))
        block = gh[first : first + count].reshape(count * NZ * OWN, WIDTH)

        def tile(j):
            features = pl.ds(pl.multiple_of(j * TILE, TILE), TILE)
            terms = lax.dot_general(
                block, w[features, :], (((1,), (1,)), ((), ())), preferred_element_type=f32
            )
            part[first : first + count, :, :, features] = terms.reshape(count, NZ, OWN, TILE)

        each(WIDTH // TILE, tile)

        slots = pl.ds(first, count)
        copy(("d", c), part.at[slots, pl.ds(theirs, 4)], swap_in.at[slots], other)

    def weight_terms(first, count, is_first, is_last):
        def tile(j):
            features = pl.ds(pl.multiple_of(j * TILE, TILE), TILE)
            tokens = xs[first : first + count, :, :, features].reshape(count * NZ * OWN, TILE)
            grads = gh[first : first + count].reshape(count * NZ * OWN, WIDTH)
            terms = lax.dot_general(
                tokens, grads, (((0,), (0,)), ((), ())), preferred_element_type=f32
            )
            if not is_first:
                terms = terms + gw[features, :]
            if is_last:
                terms = terms * factor
            gw[features, :] = terms

        each(WIDTH // TILE, tile)

    def both(slot, j):
        return part[slot, mine + j] + swap_in[slot, j]

    def swapped(c):
        arrived(("d", c))

    def x_first(dy):
        slot = slot_at(dy, 2)

        def one(j):
            x_out[dy, j // 2, 0, j] = both(slot, j).astype(bf16)

        each(4, one)
        for way in range(2):
            rows = pl.ds(2 * way, 2)
            copy(("e", dy, 0, way), x_out.at[dy, way, 0, rows], x_got.at[dy, way, 0, rows], first_near[way])

    def x_second(dy, way):
        slot = slot_at(dy, (1, 3)[way])
        arrived(("e", dy, 0, way))

        def with_got(j):
            j = j + 2 * way
            x_out[dy, way, 1, j] = (both(slot, j) + x_got[dy, way, 0, j].astype(f32)).astype(bf16)

        def without(j):
            j = j + 2 * (1 - way)
            x_out[dy, way, 1, j] = both(slot, j).astype(bf16)

        each(2, with_got)
        each(2, without)
        copy(("e", dy, 1, way), x_out.at[dy, way, 1], x_got.at[dy, way, 1], first_near[way])

    def x_last(dy):
        slot = slot_at(dy, 0)
        arrived(("e", dy, 1, 0))
        arrived(("e", dy, 1, 1))

        def one(j):
            total[dy, j] = (
                both(slot, j) + x_got[dy, 0, 1, j].astype(f32) + x_got[dy, 1, 1, j].astype(f32)
            )

        each(4, one)

    def y_first():
        def one(j):
            y_out[j // 2, 0, j] = total[2, j].astype(bf16)

        each(4, one)
        for way in range(2):
            rows = pl.ds(2 * way, 2)
            copy(("y", 0, way), y_out.at[way, 0, rows], y_got.at[way, 0, rows], second_near[way])

    def y_second(way):
        arrived(("y", 0, way))

        def with_got(j):
            j = j + 2 * way
            y_out[way, 1, j] = (total[(1, 3)[way], j] + y_got[way, 0, j].astype(f32)).astype(bf16)

        def without(j):
            j = j + 2 * (1 - way)
            y_out[way, 1, j] = total[(1, 3)[way], j].astype(bf16)

        each(2, with_got)
        each(2, without)
        copy(("y", 1, way), y_out.at[way, 1], y_got.at[way, 1], second_near[way])

    def y_last():
        arrived(("y", 1, 0))
        arrived(("y", 1, 1))

        def one(j):
            dx[j] = (
                total[0, j] + y_got[0, 1, j].astype(f32) + y_got[1, 1, j].astype(f32)
            ).astype(bf16)

        each(4, one)

    actions = dict(
        s=start, x=gather, k=spread_cot, m=forward, r=scatter, f=activate, g=spread, b=input_terms,
        w=weight_terms, d=swapped, e=x_first, h=x_second, j=x_last, u=y_first, v=y_second, z=y_last,
    )
    sent = []
    done = 0
    for event in ORDER:
        actions[event[0]](*event[1:])
        sent.append(len(copies))
        if len(sent) > SEND_LAG:
            upto = sent[-1 - SEND_LAG]
            for made in list(copies.values())[done:upto]:
                made.wait_send()
            done = upto
    for slot in range(len(SLOTS)):
        if slot != SLOT[0, 0]:
            arrived(("a", slot))
    for made in list(copies.values())[done:]:
        made.wait_send()
    act_copy.wait()


def hand_over(act, dx, gw, act_out, dx_out, gw_out, sem):
    parts = [(act, act_out, pl.ds(0, OWN)), (dx, dx_out, pl.ds(0, 4))]
    parts += [(gw, gw_out, pl.ds(j * 192, 192)) for j in range(WIDTH // 192)]
    made = [
        pltpu.make_async_copy(src.at[rows], dst.at[rows], sem.at[i])
        for i, (src, dst, rows) in enumerate(parts)
    ]
    for one in made:
        one.start()
    for one in made:
        one.wait()


def local(inputs, weight, cotangent):
    slots = NY * NX
    factor = 1.0 / math.sqrt(slots * NZ * OWN)
    shapes = (
        pltpu.VMEM((OWN, slots * WIDTH), bf16),
        pltpu.VMEM((4, OWN, WIDTH), bf16),
        pltpu.VMEM((WIDTH, WIDTH), f32),
    )
    anywhere = [pl.BlockSpec(memory_space=pl.ANY)] * 3
    act, dx, gw = pl.pallas_call(
        functools.partial(kernel, factor),
        out_shape=shapes,
        in_specs=anywhere,
        out_specs=[pl.BlockSpec(memory_space=pltpu.VMEM)] * 3,
        scratch_shapes=[
            pltpu.VMEM((slots, NZ, OWN, WIDTH), bf16),
            pltpu.VMEM((slots, NZ, OWN, WIDTH), bf16),
            pltpu.VMEM((WIDTH, WIDTH), bf16),
            pltpu.VMEM((slots, OWN, WIDTH), bf16),
            pltpu.VMEM((slots, NZ, OWN, WIDTH), f32),
            pltpu.VMEM((2, 4, slots, OWN, WIDTH), bf16),
            pltpu.VMEM((2, 4, slots, OWN, WIDTH), bf16),
            pltpu.VMEM((slots, OWN, WIDTH), bf16),
            pltpu.VMEM((slots, 4, OWN, WIDTH), f32),
            pltpu.VMEM((NY, 2, 2, 4, OWN, WIDTH), bf16),
            pltpu.VMEM((NY, 2, 2, 4, OWN, WIDTH), bf16),
            pltpu.VMEM((NY, 4, OWN, WIDTH), f32),
            pltpu.VMEM((2, 2, 4, OWN, WIDTH), bf16),
            pltpu.VMEM((2, 2, 4, OWN, WIDTH), bf16),
            pltpu.SemaphoreType.DMA((COPIES,)),
            pltpu.SemaphoreType.DMA((COPIES,)),
            pltpu.SemaphoreType.DMA((4,)),
        ],
        compiler_params=pltpu.CompilerParams(
            collective_id=0, has_side_effects=True, vmem_limit_bytes=56 * 2**20
        ),
        cost_estimate=pl.CostEstimate(flops=7 * 10**9, bytes_accessed=10**7, transcendentals=2 * 10**5),
    )(inputs.reshape(4, OWN, WIDTH), weight[0], cotangent)
    act, dx, gw = pl.pallas_call(
        hand_over,
        out_shape=[jax.ShapeDtypeStruct(one.shape, one.dtype) for one in shapes],
        in_specs=anywhere,
        out_specs=anywhere,
        scratch_shapes=[pltpu.SemaphoreType.DMA((2 + WIDTH // 192,))],
    )(*(pltpu.with_memory_space_constraint(one, pltpu.VMEM) for one in (act, dx, gw)))
    return (act, dx.reshape(4 * OWN, WIDTH), gw[None])


def solution(mesh):
    in_specs = (P(("depth", "col"), "row"), P("col", "row", "depth"), P(("depth", "row"), "col"))
    out_specs = (P(("depth", "row"), "col"), P(("depth", "col"), "row"), P("col", "row", "depth"))
    return jax.shard_map(local, mesh=mesh, in_specs=in_specs, out_specs=out_specs, check_vma=False)
```

```python
import functools
import math

import jax
import jax.numpy as jnp
from jax import lax
from jax.experimental import pallas as pl
from jax.experimental.pallas import tpu as pltpu
from jax.sharding import PartitionSpec as P

MESH = pl.DeviceIdType.MESH
slope_c = math.sqrt(2.0 / math.pi)
bf16, f32 = jnp.bfloat16, jnp.float32
NY, NX, NZ, NC = 4, 4, 8, 2
OWN = 16
WIDTH = 768
HALF = WIDTH // 2
TILE = 256
SEND_LAG = 24

SLOTS = (
    (3, 2), (1, 1), (3, 3), (2, 2), (2, 3), (1, 2), (2, 1), (1, 3),
    (2, 0), (3, 1), (0, 2), (0, 1), (1, 0), (3, 0), (0, 3), (0, 0),
)
CHUNKS = (
    (0, 2), (2, 1), (3, 1), (4, 3), (7, 1), (8, 1), (9, 2), (11, 2),
    (13, 2), (15, 1),
)
COPIES = 296
FIRST = 9
ORDER = (
    ("s",), ("m", 9, 1), ("r", 9, 0), ("x", 0, 3), ("x", 3, 0), ("x", 1, 0),
    ("x", 0, 1), ("r", 9, 1), ("m", 7, 2), ("r", 8, 0), ("r", 7, 0), ("x", 3, 3),
    ("x", 1, 3), ("x", 2, 0), ("k", 3, 3), ("x", 0, 2), ("r", 9, 2), ("m", 1, 1),
    ("x", 3, 1), ("r", 1, 0), ("x", 1, 1), ("r", 8, 1), ("m", 5, 1), ("r", 5, 0),
    ("r", 7, 1), ("m", 6, 1), ("r", 6, 0), ("x", 3, 2), ("r", 9, 3), ("x", 2, 3),
    ("r", 1, 1), ("m", 4, 1), ("r", 4, 0), ("x", 2, 1), ("r", 8, 2), ("x", 1, 2),
    ("r", 5, 1), ("k", 0, 2), ("k", 3, 2), ("m", 0, 1), ("r", 0, 0), ("r", 6, 1),
    ("m", 3, 1), ("r", 3, 0), ("k", 0, 3), ("r", 4, 1), ("x", 2, 2), ("r", 1, 2),
    ("k", 2, 0), ("k", 3, 1), ("r", 7, 2), ("k", 2, 3), ("k", 2, 2), ("k", 1, 2),
    ("m", 2, 1), ("r", 2, 0), ("r", 0, 1), ("r", 6, 2), ("r", 3, 1), ("r", 4, 2),
    ("r", 2, 1), ("r", 5, 2), ("k", 2, 1), ("r", 6, 3), ("k", 1, 3), ("r", 0, 2),
    ("r", 4, 3), ("k", 3, 0), ("r", 3, 2), ("r", 2, 2), ("f", 6), ("k", 0, 1),
    ("r", 5, 3), ("r", 7, 3), ("r", 0, 3), ("r", 2, 3), ("k", 1, 1), ("r", 3, 3),
    ("f", 4), ("f", 7), ("f", 0), ("r", 8, 3), ("k", 1, 0), ("f", 2),
    ("f", 3), ("g", 4, 1), ("f", 5), ("g", 0, 1), ("r", 1, 3), ("g", 2, 1),
    ("g", 3, 1), ("g", 6, 1), ("g", 5, 1), ("g", 2, 2), ("g", 0, 2), ("g", 3, 2),
    ("f", 1), ("g", 2, 3), ("g", 4, 2), ("f", 8), ("g", 5, 2), ("g", 3, 3),
    ("g", 0, 3), ("g", 1, 1), ("g", 6, 2), ("t",), ("b", 2, 1), ("g", 7, 1),
    ("g", 8, 1), ("d", 2), ("f", 9), ("e", 2), ("b", 3, 1), ("g", 1, 2),
    ("g", 4, 3), ("g", 5, 3), ("b", 0, 1), ("g", 6, 3), ("g", 7, 2), ("w", 0, 2, 1, 0),
    ("g", 8, 2), ("d", 3), ("e", 1), ("d", 0), ("h", 2, 1), ("g", 1, 3),
    ("g", 9, 1), ("e", 3), ("h", 2, 0), ("b", 4, 3), ("g", 7, 3), ("h", 1, 0),
    ("g", 8, 3), ("b", 1, 1), ("g", 9, 2), ("d", 4), ("h", 1, 1), ("j", 2),
    ("e", 0), ("u",), ("h", 3, 0), ("d", 1), ("h", 3, 1), ("b", 7, 1),
    ("b", 8, 1), ("g", 9, 3), ("d", 7), ("d", 8), ("h", 0, 1), ("h", 0, 0),
    ("j", 1), ("v", 0), ("j", 3), ("v", 1), ("b", 9, 1), ("w", 2, 14, 0, 1),
    ("d", 9), ("j", 0), ("z",),
)
SLOT = {name: index for index, name in enumerate(SLOTS)}


def gelu_both(h):
    t = jnp.tanh(slope_c * (h + 0.044715 * h * h * h))
    value = 0.5 * h * (1.0 + t)
    slope = 0.5 * (1.0 + t) + 0.5 * h * (1.0 - t * t) * slope_c * (1.0 + 3.0 * 0.044715 * h * h)
    return value, slope


def kernel(
    factor, x_in, w_in, cot_in, act_out, dx, gw,
    xs, gh, w, w_turned, cot, part, ring_out, ring_in, act, swap_in, x_out, x_got, total, y_out, y_got,
    send_sem, recv_sem, local_sem,
):
    depth, row, col = lax.axis_index("depth"), lax.axis_index("row"), lax.axis_index("col")
    y, x = depth // NX, lax.rem(depth, NX)

    def at_depth(dy, dx):
        return lax.rem(y + dy, NY) * NX + lax.rem(x + dx, NX)

    def near(dy, dx):
        return (at_depth(dy, dx), row, col)

    def along_z(distance):
        return (depth, lax.rem(row + NZ + distance, NZ), col)

    z_near = (along_z(1), along_z(-1))
    first_near = (near(col, 1 - col), near(3 * col, 3 - 3 * col))
    second_near = (near(1 - col, col), near(3 - 3 * col, 3 * col))

    def slot_at(second, first):
        there, turned = SLOT[second, first], SLOT[first, second]
        return there if there == turned else there + col * (turned - there)

    other = (depth, row, 1 - col)
    copies, index_of = {}, {}

    def copy(name, src, dst, device):
        index = len(index_of)
        index_of[name] = index
        made = pltpu.make_async_remote_copy(
            src_ref=src, dst_ref=dst, send_sem=send_sem.at[index], recv_sem=recv_sem.at[index],
            device_id=device, device_id_type=MESH,
        )
        copies[name] = made
        made.start()

    waited = set()

    def arrived(name):
        if name not in waited:
            copies[name].wait_recv()
            waited.add(name)

    def each(count, body):
        def step(j, carry):
            body(j)
            return carry
        lax.fori_loop(0, count, step, 0)

    mine = pl.multiple_of(col * 4, 4)
    theirs = pl.multiple_of(4 - col * 4, 4)

    def inputs_to_core(second, first):
        block = xs.at[slot_at(second, first), pl.ds(mine, 4)]
        copy(("xc", second, first), block, block, other)

    here = pl.ds(pl.multiple_of(depth * WIDTH, WIDTH), WIDTH)
    w_copy = pltpu.make_async_copy(w_in, w, local_sem.at[1])
    cot_copy = pltpu.make_async_copy(cot_in.at[:, here], cot.at[SLOT[0, 0]], local_sem.at[2])
    act_copy = pltpu.make_async_copy(act.at[SLOT[0, 0]], act_out.at[:, here], local_sem.at[3])

    def start():
        barrier = pltpu.get_barrier_semaphore()
        peers = [*first_near, *second_near, other, *z_near]
        block = xs.at[SLOT[0, 0], pl.ds(mine, 4)]
        own = pltpu.make_async_copy(x_in, block, local_sem.at[0])
        own.start()
        w_copy.start()
        cot_copy.start()
        for peer in peers:
            pl.semaphore_signal(barrier, inc=1, device_id=peer, device_id_type=MESH)
        own.wait()
        pl.semaphore_wait(barrier, len(peers))
        for (dy, dx), device in (((0, 3), first_near[0]), ((0, 1), first_near[1]), ((3, 0), second_near[0]), ((1, 0), second_near[1])):
            copy(("x", dy, dx), block, xs.at[slot_at(dy, dx), pl.ds(mine, 4)], device)
        inputs_to_core(0, 0)

    def half_of(slot, half):
        return xs.at[slot, pl.ds(pl.multiple_of(col * 4 + 2 * half, 2), 2)]

    def gather(second, first):
        slot = slot_at(second, first)
        whole = xs.at[slot, pl.ds(mine, 4)]
        if first == 2 and second == 0 or second == 2:
            arrived(("xh", second, first, 0))
            arrived(("xh", second, first, 1))
        else:
            arrived(("x", second, first))
        if second == 0:
            if first == 3:
                copy(("xh", 0, 2, 0), half_of(slot, 0), half_of(slot_at(0, 2), 0), first_near[0])
            if first == 1:
                copy(("xh", 0, 2, 1), half_of(slot, 1), half_of(slot_at(0, 2), 1), first_near[1])
            copy(("x", 3, first), whole, xs.at[slot_at(3, first), pl.ds(mine, 4)], second_near[0])
            copy(("x", 1, first), whole, xs.at[slot_at(1, first), pl.ds(mine, 4)], second_near[1])
        if second == 3:
            copy(("xh", 2, first, 0), half_of(slot, 0), half_of(slot_at(2, first), 0), second_near[0])
        if second == 1:
            copy(("xh", 2, first, 1), half_of(slot, 1), half_of(slot_at(2, first), 1), second_near[1])
        inputs_to_core(second, first)

    def spread_cot(dy, dx):
        block = cot_in.at[:, pl.ds(pl.multiple_of(at_depth(dy, dx) * WIDTH, WIDTH), WIDTH)]
        slot = SLOT[(4 - dy) % 4, (4 - dx) % 4]
        copy(("k", slot), block, cot.at[slot], near(dy, dx))

    def forward(c, chunks):
        first, count = CHUNKS[c][0], sum(CHUNKS[c + i][1] for i in range(chunks))
        if c == FIRST:
            w_copy.wait()
        for slot in range(first, first + count):
            dy, dx = SLOTS[slot]
            arrived(("xc", dy, dx))
            arrived(("xc", dx, dy))
        block = xs[first : first + count].reshape(count * NZ * OWN, WIDTH)

        def tile(j):
            columns = pl.ds(pl.multiple_of(j * TILE, TILE), TILE)
            terms = jnp.dot(block, w[:, columns], preferred_element_type=f32)
            part[first : first + count, :, :, columns] = terms.reshape(count, NZ, OWN, TILE)

        each(WIDTH // TILE, tile)

    def scatter(c, step):
        first, count = CHUNKS[c]
        slots = pl.ds(first, count)
        for way in range(2):
            owner = lax.rem(row + (4 - step if way == 0 else 4 + step), NZ)
            halves = (slice(0, HALF), slice(HALF, WIDTH))
            if step > 0:
                arrived(("r", c, step - 1, way))

            def add(j):
                s = first + j
                if step == 0:
                    cols = halves[way]
                    ring_out[way, 0, s, :, cols] = part[s, owner, :, cols].astype(bf16)
                elif step == 1:
                    cols, rest = halves[way], halves[1 - way]
                    got = ring_in[way, 0, s, :, cols].astype(f32)
                    ring_out[way, 1, s, :, cols] = (part[s, owner, :, cols] + got).astype(bf16)
                    ring_out[way, 1, s, :, rest] = part[s, owner, :, rest].astype(bf16)
                else:
                    got = ring_in[way, step - 1, s].astype(f32)
                    ring_out[way, step, s] = (part[s, owner] + got).astype(bf16)

            each(count, add)
            cols = halves[way] if step == 0 else slice(0, WIDTH)
            copy(
                ("r", c, step, way), ring_out.at[way, step, slots, :, cols],
                ring_in.at[way, step, slots, :, cols], z_near[way],
            )

    def activate(c):
        first, count = CHUNKS[c]
        arrived(("r", c, 3, 0))
        arrived(("r", c, 3, 1))
        for slot in range(first, first + count):
            if slot != SLOT[0, 0]:
                arrived(("k", slot))
            else:
                cot_copy.wait()

        def one(j):
            s = first + j
            h = part[s, row] + ring_in[0, 3, s].astype(f32) + ring_in[1, 3, s].astype(f32)
            value, slope = gelu_both(h)
            act[s] = value.astype(bf16)
            gh[s, row] = (cot[s].astype(f32) * slope).astype(bf16)

        each(count, one)
        spread(c, 0)
        for slot in range(first, first + count):
            if slot == SLOT[0, 0]:
                act_copy.start()
            else:
                copy(("a", slot), act.at[slot], act_out.at[:, here], near(*SLOTS[slot]))

    def spread(c, step):
        first, count = CHUNKS[c]
        slots = pl.ds(first, count)
        for way in range(2):
            if step > 0:
                arrived(("g", c, step - 1, way))
            owner = lax.rem(row + (NZ - step if way == 0 else step), NZ)
            cols = slice(0, WIDTH) if step < 3 else (slice(0, HALF), slice(HALF, WIDTH))[way]
            block = gh.at[slots, owner, :, cols]
            copy(("g", c, step, way), block, block, z_near[way])

    def turn():
        def tile(j):
            features = pl.ds(pl.multiple_of(j * TILE, TILE), TILE)
            w_turned[:, features] = w[features, :].T

        each(WIDTH // TILE, tile)

    def input_terms(c, chunks):
        first, count = CHUNKS[c][0], sum(CHUNKS[c + i][1] for i in range(chunks))
        for i in range(c, c + chunks):
            arrived(("g", i, 3, 0))
            arrived(("g", i, 3, 1))
        block = gh[first : first + count].reshape(count * NZ * OWN, WIDTH)

        def tile(j):
            features = pl.ds(pl.multiple_of(j * TILE, TILE), TILE)
            terms = jnp.dot(block, w_turned[:, features], preferred_element_type=f32)
            part[first : first + count, :, :, features] = terms.reshape(count, NZ, OWN, TILE)

        each(WIDTH // TILE, tile)

        slots = pl.ds(first, count)
        copy(("d", c), part.at[slots, pl.ds(theirs, 4)], swap_in.at[slots], other)

    def weight_terms(first, count, is_first, is_last):
        def tile(j):
            features = pl.ds(pl.multiple_of(j * TILE, TILE), TILE)
            tokens = xs[first : first + count, :, :, features].reshape(count * NZ * OWN, TILE)
            grads = gh[first : first + count].reshape(count * NZ * OWN, WIDTH)
            terms = lax.dot_general(
                tokens, grads, (((0,), (0,)), ((), ())), preferred_element_type=f32
            )
            if not is_first:
                terms = terms + gw[features, :]
            if is_last:
                terms = terms * factor
            gw[features, :] = terms

        each(WIDTH // TILE, tile)

    def both(slot, j):
        return part[slot, mine + j] + swap_in[slot, j]

    def swapped(c):
        arrived(("d", c))

    def x_first(dy):
        slot = slot_at(dy, 2)

        def one(j):
            x_out[dy, j // 2, 0, j] = both(slot, j).astype(bf16)

        each(4, one)
        for way in range(2):
            rows = pl.ds(2 * way, 2)
            copy(("e", dy, 0, way), x_out.at[dy, way, 0, rows], x_got.at[dy, way, 0, rows], first_near[way])

    def x_second(dy, way):
        slot = slot_at(dy, (1, 3)[way])
        arrived(("e", dy, 0, way))

        def with_got(j):
            j = j + 2 * way
            x_out[dy, way, 1, j] = (both(slot, j) + x_got[dy, way, 0, j].astype(f32)).astype(bf16)

        def without(j):
            j = j + 2 * (1 - way)
            x_out[dy, way, 1, j] = both(slot, j).astype(bf16)

        each(2, with_got)
        each(2, without)
        copy(("e", dy, 1, way), x_out.at[dy, way, 1], x_got.at[dy, way, 1], first_near[way])

    def x_last(dy):
        slot = slot_at(dy, 0)
        arrived(("e", dy, 1, 0))
        arrived(("e", dy, 1, 1))

        def one(j):
            total[dy, j] = (
                both(slot, j) + x_got[dy, 0, 1, j].astype(f32) + x_got[dy, 1, 1, j].astype(f32)
            )

        each(4, one)

    def y_first():
        def one(j):
            y_out[j // 2, 0, j] = total[2, j].astype(bf16)

        each(4, one)
        for way in range(2):
            rows = pl.ds(2 * way, 2)
            copy(("y", 0, way), y_out.at[way, 0, rows], y_got.at[way, 0, rows], second_near[way])

    def y_second(way):
        arrived(("y", 0, way))

        def with_got(j):
            j = j + 2 * way
            y_out[way, 1, j] = (total[(1, 3)[way], j] + y_got[way, 0, j].astype(f32)).astype(bf16)

        def without(j):
            j = j + 2 * (1 - way)
            y_out[way, 1, j] = total[(1, 3)[way], j].astype(bf16)

        each(2, with_got)
        each(2, without)
        copy(("y", 1, way), y_out.at[way, 1], y_got.at[way, 1], second_near[way])

    def y_last():
        arrived(("y", 1, 0))
        arrived(("y", 1, 1))

        def one(j):
            dx[j] = (
                total[0, j] + y_got[0, 1, j].astype(f32) + y_got[1, 1, j].astype(f32)
            ).astype(bf16)

        each(4, one)

    actions = dict(
        s=start, x=gather, k=spread_cot, m=forward, r=scatter, f=activate, g=spread, b=input_terms, t=turn,
        w=weight_terms, d=swapped, e=x_first, h=x_second, j=x_last, u=y_first, v=y_second, z=y_last,
    )
    sent = []
    done = 0
    for event in ORDER:
        actions[event[0]](*event[1:])
        sent.append(len(copies))
        if len(sent) > SEND_LAG:
            upto = sent[-1 - SEND_LAG]
            for made in list(copies.values())[done:upto]:
                made.wait_send()
            done = upto
    for slot in range(len(SLOTS)):
        if slot != SLOT[0, 0]:
            arrived(("a", slot))
    for made in list(copies.values())[done:]:
        made.wait_send()
    act_copy.wait()


def hand_over(act, dx, gw, act_out, dx_out, gw_out, sem):
    parts = [(act, act_out, pl.ds(0, OWN)), (dx, dx_out, pl.ds(0, 4))]
    parts += [(gw, gw_out, pl.ds(j * 96, 96)) for j in range(WIDTH // 96)]
    made = [
        pltpu.make_async_copy(src.at[rows], dst.at[rows], sem.at[i])
        for i, (src, dst, rows) in enumerate(parts)
    ]
    for one in made:
        one.start()
    for one in made:
        one.wait()


def local(inputs, weight, cotangent):
    slots = NY * NX
    factor = 1.0 / math.sqrt(slots * NZ * OWN)
    shapes = (
        pltpu.VMEM((OWN, slots * WIDTH), bf16),
        pltpu.VMEM((4, OWN, WIDTH), bf16),
        pltpu.VMEM((WIDTH, WIDTH), f32),
    )
    anywhere = [pl.BlockSpec(memory_space=pl.ANY)] * 3
    act, dx, gw = pl.pallas_call(
        functools.partial(kernel, factor),
        out_shape=shapes,
        in_specs=anywhere,
        out_specs=[pl.BlockSpec(memory_space=pltpu.VMEM)] * 3,
        scratch_shapes=[
            pltpu.VMEM((slots, NZ, OWN, WIDTH), bf16),
            pltpu.VMEM((slots, NZ, OWN, WIDTH), bf16),
            pltpu.VMEM((WIDTH, WIDTH), bf16),
            pltpu.VMEM((WIDTH, WIDTH), bf16),
            pltpu.VMEM((slots, OWN, WIDTH), bf16),
            pltpu.VMEM((slots, NZ, OWN, WIDTH), f32),
            pltpu.VMEM((2, 4, slots, OWN, WIDTH), bf16),
            pltpu.VMEM((2, 4, slots, OWN, WIDTH), bf16),
            pltpu.VMEM((slots, OWN, WIDTH), bf16),
            pltpu.VMEM((slots, 4, OWN, WIDTH), f32),
            pltpu.VMEM((NY, 2, 2, 4, OWN, WIDTH), bf16),
            pltpu.VMEM((NY, 2, 2, 4, OWN, WIDTH), bf16),
            pltpu.VMEM((NY, 4, OWN, WIDTH), f32),
            pltpu.VMEM((2, 2, 4, OWN, WIDTH), bf16),
            pltpu.VMEM((2, 2, 4, OWN, WIDTH), bf16),
            pltpu.SemaphoreType.DMA((COPIES,)),
            pltpu.SemaphoreType.DMA((COPIES,)),
            pltpu.SemaphoreType.DMA((4,)),
        ],
        compiler_params=pltpu.CompilerParams(
            collective_id=0, has_side_effects=True, vmem_limit_bytes=56 * 2**20
        ),
        cost_estimate=pl.CostEstimate(flops=7 * 10**9, bytes_accessed=10**7, transcendentals=2 * 10**5),
    )(inputs.reshape(4, OWN, WIDTH), weight[0], cotangent)
    act, dx, gw = pl.pallas_call(
        hand_over,
        out_shape=[jax.ShapeDtypeStruct(one.shape, one.dtype) for one in shapes],
        in_specs=anywhere,
        out_specs=anywhere,
        scratch_shapes=[pltpu.SemaphoreType.DMA((2 + WIDTH // 96,))],
    )(*(pltpu.with_memory_space_constraint(one, pltpu.VMEM) for one in (act, dx, gw)))
    return (act, dx.reshape(4 * OWN, WIDTH), gw[None])


def solution(mesh):
    in_specs = (P(("depth", "col"), "row"), P("col", "row", "depth"), P(("depth", "row"), "col"))
    out_specs = (P(("depth", "row"), "col"), P(("depth", "col"), "row"), P("col", "row", "depth"))
    return jax.shard_map(local, mesh=mesh, in_specs=in_specs, out_specs=out_specs, check_vma=False)
```

```python
import functools
import math

import jax
import jax.numpy as jnp
from jax import lax
from jax.experimental import pallas as pl
from jax.experimental.pallas import tpu as pltpu
from jax.sharding import PartitionSpec as P

MESH = pl.DeviceIdType.MESH
slope_c = math.sqrt(2.0 / math.pi)
bf16, f32 = jnp.bfloat16, jnp.float32
NY, NX, NZ, NC = 4, 4, 8, 2
OWN = 16
WIDTH = 768
HALF = WIDTH // 2
TILE = 256
SEND_LAG = 24

SLOTS = (
    (3, 2), (1, 1), (3, 3), (2, 2), (2, 3), (1, 2), (2, 1), (1, 3),
    (2, 0), (3, 1), (0, 2), (0, 1), (1, 0), (3, 0), (0, 3), (0, 0),
)
CHUNKS = (
    (0, 2), (2, 1), (3, 1), (4, 3), (7, 1), (8, 1), (9, 2), (11, 2),
    (13, 2), (15, 1),
)
COPIES = 296
FIRST = 9
ORDER = (
    ("s",), ("m", 9, 1), ("r", 9, 0), ("x", 0, 3), ("x", 3, 0), ("x", 1, 0),
    ("x", 0, 1), ("r", 9, 1), ("m", 7, 2), ("r", 8, 0), ("r", 7, 0), ("x", 3, 3),
    ("x", 1, 3), ("x", 2, 0), ("k", 3, 3), ("x", 0, 2), ("r", 9, 2), ("m", 1, 1),
    ("x", 3, 1), ("r", 1, 0), ("x", 1, 1), ("r", 8, 1), ("m", 5, 1), ("r", 5, 0),
    ("r", 7, 1), ("m", 6, 1), ("r", 6, 0), ("x", 3, 2), ("r", 9, 3), ("x", 2, 3),
    ("r", 1, 1), ("m", 4, 1), ("r", 4, 0), ("x", 2, 1), ("r", 8, 2), ("x", 1, 2),
    ("r", 5, 1), ("k", 0, 2), ("k", 3, 2), ("m", 0, 1), ("r", 0, 0), ("r", 6, 1),
    ("m", 3, 1), ("r", 3, 0), ("k", 0, 3), ("r", 4, 1), ("x", 2, 2), ("r", 1, 2),
    ("k", 2, 0), ("k", 3, 1), ("r", 7, 2), ("k", 2, 3), ("k", 2, 2), ("k", 1, 2),
    ("m", 2, 1), ("r", 2, 0), ("r", 0, 1), ("r", 6, 2), ("r", 3, 1), ("r", 4, 2),
    ("r", 2, 1), ("r", 5, 2), ("k", 2, 1), ("r", 6, 3), ("k", 1, 3), ("r", 0, 2),
    ("r", 4, 3), ("k", 3, 0), ("r", 3, 2), ("r", 2, 2), ("f", 6), ("k", 0, 1),
    ("r", 5, 3), ("r", 7, 3), ("r", 0, 3), ("r", 2, 3), ("k", 1, 1), ("r", 3, 3),
    ("f", 4), ("f", 7), ("f", 0), ("r", 8, 3), ("k", 1, 0), ("f", 2),
    ("f", 3), ("g", 4, 1), ("f", 5), ("g", 0, 1), ("r", 1, 3), ("g", 2, 1),
    ("g", 3, 1), ("g", 6, 1), ("g", 5, 1), ("g", 2, 2), ("g", 0, 2), ("g", 3, 2),
    ("f", 1), ("g", 2, 3), ("g", 4, 2), ("f", 8), ("g", 5, 2), ("g", 3, 3),
    ("g", 0, 3), ("g", 1, 1), ("g", 6, 2), ("t",), ("b", 2, 1), ("g", 7, 1),
    ("g", 8, 1), ("d", 2), ("f", 9), ("e", 2), ("b", 3, 1), ("g", 1, 2),
    ("g", 4, 3), ("g", 5, 3), ("b", 0, 1), ("g", 6, 3), ("g", 7, 2), ("w", 0, 2, 1, 0),
    ("g", 8, 2), ("d", 3), ("e", 1), ("d", 0), ("h", 2, 1), ("g", 1, 3),
    ("g", 9, 1), ("e", 3), ("h", 2, 0), ("b", 4, 3), ("g", 7, 3), ("h", 1, 0),
    ("g", 8, 3), ("b", 1, 1), ("g", 9, 2), ("d", 4), ("h", 1, 1), ("j", 2),
    ("e", 0), ("u",), ("h", 3, 0), ("d", 1), ("h", 3, 1), ("b", 7, 2),
    ("g", 9, 3), ("d", 7), ("h", 0, 1), ("h", 0, 0), ("j", 1), ("v", 0),
    ("j", 3), ("v", 1), ("b", 9, 1), ("w", 2, 14, 0, 1), ("d", 9), ("j", 0),
    ("z",),
)
SLOT = {name: index for index, name in enumerate(SLOTS)}


def gelu_both(h):
    t = jnp.tanh(slope_c * (h + 0.044715 * h * h * h))
    value = 0.5 * h * (1.0 + t)
    slope = 0.5 * (1.0 + t) + 0.5 * h * (1.0 - t * t) * slope_c * (1.0 + 3.0 * 0.044715 * h * h)
    return value, slope


def kernel(
    factor, x_in, w_in, cot_in, act_out, dx, gw,
    xs, gh, w, w_turned, cot, part, ring_out, ring_in, act, swap_in, x_out, x_got, total, y_out, y_got,
    send_sem, recv_sem, local_sem,
):
    depth, row, col = lax.axis_index("depth"), lax.axis_index("row"), lax.axis_index("col")
    y, x = depth // NX, lax.rem(depth, NX)

    def at_depth(dy, dx):
        return lax.rem(y + dy, NY) * NX + lax.rem(x + dx, NX)

    def near(dy, dx):
        return (at_depth(dy, dx), row, col)

    def along_z(distance):
        return (depth, lax.rem(row + NZ + distance, NZ), col)

    z_near = (along_z(1), along_z(-1))
    first_near = (near(col, 1 - col), near(3 * col, 3 - 3 * col))
    second_near = (near(1 - col, col), near(3 - 3 * col, 3 * col))

    def slot_at(second, first):
        there, turned = SLOT[second, first], SLOT[first, second]
        return there if there == turned else there + col * (turned - there)

    other = (depth, row, 1 - col)
    copies, index_of = {}, {}

    def copy(name, src, dst, device):
        index = len(index_of)
        index_of[name] = index
        made = pltpu.make_async_remote_copy(
            src_ref=src, dst_ref=dst, send_sem=send_sem.at[index], recv_sem=recv_sem.at[index],
            device_id=device, device_id_type=MESH,
        )
        copies[name] = made
        made.start()

    waited = set()

    def arrived(name):
        if name not in waited:
            copies[name].wait_recv()
            waited.add(name)

    def each(count, body):
        def step(j, carry):
            body(j)
            return carry
        lax.fori_loop(0, count, step, 0)

    mine = pl.multiple_of(col * 4, 4)
    theirs = pl.multiple_of(4 - col * 4, 4)

    def inputs_to_core(second, first):
        block = xs.at[slot_at(second, first), pl.ds(mine, 4)]
        copy(("xc", second, first), block, block, other)

    here = pl.ds(pl.multiple_of(depth * WIDTH, WIDTH), WIDTH)
    w_copy = pltpu.make_async_copy(w_in, w, local_sem.at[1])
    cot_copy = pltpu.make_async_copy(cot_in.at[:, here], cot.at[SLOT[0, 0]], local_sem.at[2])
    act_copy = pltpu.make_async_copy(act.at[SLOT[0, 0]], act_out.at[:, here], local_sem.at[3])

    def start():
        barrier = pltpu.get_barrier_semaphore()
        peers = [*first_near, *second_near, other, *z_near]
        block = xs.at[SLOT[0, 0], pl.ds(mine, 4)]
        own = pltpu.make_async_copy(x_in, block, local_sem.at[0])
        own.start()
        w_copy.start()
        cot_copy.start()
        for peer in peers:
            pl.semaphore_signal(barrier, inc=1, device_id=peer, device_id_type=MESH)
        own.wait()
        pl.semaphore_wait(barrier, len(peers))
        for (dy, dx), device in (((0, 3), first_near[0]), ((0, 1), first_near[1]), ((3, 0), second_near[0]), ((1, 0), second_near[1])):
            copy(("x", dy, dx), block, xs.at[slot_at(dy, dx), pl.ds(mine, 4)], device)
        inputs_to_core(0, 0)

    def half_of(slot, half):
        return xs.at[slot, pl.ds(pl.multiple_of(col * 4 + 2 * half, 2), 2)]

    def gather(second, first):
        slot = slot_at(second, first)
        whole = xs.at[slot, pl.ds(mine, 4)]
        if first == 2 and second == 0 or second == 2:
            arrived(("xh", second, first, 0))
            arrived(("xh", second, first, 1))
        else:
            arrived(("x", second, first))
        if second == 0:
            if first == 3:
                copy(("xh", 0, 2, 0), half_of(slot, 0), half_of(slot_at(0, 2), 0), first_near[0])
            if first == 1:
                copy(("xh", 0, 2, 1), half_of(slot, 1), half_of(slot_at(0, 2), 1), first_near[1])
            copy(("x", 3, first), whole, xs.at[slot_at(3, first), pl.ds(mine, 4)], second_near[0])
            copy(("x", 1, first), whole, xs.at[slot_at(1, first), pl.ds(mine, 4)], second_near[1])
        if second == 3:
            copy(("xh", 2, first, 0), half_of(slot, 0), half_of(slot_at(2, first), 0), second_near[0])
        if second == 1:
            copy(("xh", 2, first, 1), half_of(slot, 1), half_of(slot_at(2, first), 1), second_near[1])
        inputs_to_core(second, first)

    def spread_cot(dy, dx):
        block = cot_in.at[:, pl.ds(pl.multiple_of(at_depth(dy, dx) * WIDTH, WIDTH), WIDTH)]
        slot = SLOT[(4 - dy) % 4, (4 - dx) % 4]
        copy(("k", slot), block, cot.at[slot], near(dy, dx))

    def forward(c, chunks):
        first, count = CHUNKS[c][0], sum(CHUNKS[c + i][1] for i in range(chunks))
        if c == FIRST:
            w_copy.wait()
        for slot in range(first, first + count):
            dy, dx = SLOTS[slot]
            arrived(("xc", dy, dx))
            arrived(("xc", dx, dy))
        block = xs[first : first + count].reshape(count * NZ * OWN, WIDTH)

        def tile(j):
            columns = pl.ds(pl.multiple_of(j * TILE, TILE), TILE)
            terms = jnp.dot(block, w[:, columns], preferred_element_type=f32)
            part[first : first + count, :, :, columns] = terms.reshape(count, NZ, OWN, TILE)

        each(WIDTH // TILE, tile)

    def scatter(c, step):
        first, count = CHUNKS[c]
        slots = pl.ds(first, count)
        for way in range(2):
            owner = lax.rem(row + (4 - step if way == 0 else 4 + step), NZ)
            halves = (slice(0, HALF), slice(HALF, WIDTH))
            if step > 0:
                arrived(("r", c, step - 1, way))

            def add(j):
                s = first + j
                if step == 0:
                    cols = halves[way]
                    ring_out[way, 0, s, :, cols] = part[s, owner, :, cols].astype(bf16)
                elif step == 1:
                    cols, rest = halves[way], halves[1 - way]
                    got = ring_in[way, 0, s, :, cols].astype(f32)
                    ring_out[way, 1, s, :, cols] = (part[s, owner, :, cols] + got).astype(bf16)
                    ring_out[way, 1, s, :, rest] = part[s, owner, :, rest].astype(bf16)
                else:
                    got = ring_in[way, step - 1, s].astype(f32)
                    ring_out[way, step, s] = (part[s, owner] + got).astype(bf16)

            each(count, add)
            cols = halves[way] if step == 0 else slice(0, WIDTH)
            copy(
                ("r", c, step, way), ring_out.at[way, step, slots, :, cols],
                ring_in.at[way, step, slots, :, cols], z_near[way],
            )

    def activate(c):
        first, count = CHUNKS[c]
        arrived(("r", c, 3, 0))
        arrived(("r", c, 3, 1))
        for slot in range(first, first + count):
            if slot != SLOT[0, 0]:
                arrived(("k", slot))
            else:
                cot_copy.wait()

        def one(j):
            s = first + j
            h = part[s, row] + ring_in[0, 3, s].astype(f32) + ring_in[1, 3, s].astype(f32)
            value, slope = gelu_both(h)
            act[s] = value.astype(bf16)
            gh[s, row] = (cot[s].astype(f32) * slope).astype(bf16)

        each(count, one)
        spread(c, 0)
        for slot in range(first, first + count):
            if slot == SLOT[0, 0]:
                act_copy.start()
            else:
                copy(("a", slot), act.at[slot], act_out.at[:, here], near(*SLOTS[slot]))

    def spread(c, step):
        first, count = CHUNKS[c]
        slots = pl.ds(first, count)
        for way in range(2):
            if step > 0:
                arrived(("g", c, step - 1, way))
            owner = lax.rem(row + (NZ - step if way == 0 else step), NZ)
            cols = slice(0, WIDTH) if step < 3 else (slice(0, HALF), slice(HALF, WIDTH))[way]
            block = gh.at[slots, owner, :, cols]
            copy(("g", c, step, way), block, block, z_near[way])

    def turn():
        def tile(j):
            features = pl.ds(pl.multiple_of(j * TILE, TILE), TILE)
            w_turned[:, features] = w[features, :].T

        each(WIDTH // TILE, tile)

    def input_terms(c, chunks):
        first, count = CHUNKS[c][0], sum(CHUNKS[c + i][1] for i in range(chunks))
        for i in range(c, c + chunks):
            arrived(("g", i, 3, 0))
            arrived(("g", i, 3, 1))
        block = gh[first : first + count].reshape(count * NZ * OWN, WIDTH)

        def tile(j):
            features = pl.ds(pl.multiple_of(j * TILE, TILE), TILE)
            terms = jnp.dot(block, w_turned[:, features], preferred_element_type=f32)
            part[first : first + count, :, :, features] = terms.reshape(count, NZ, OWN, TILE)

        each(WIDTH // TILE, tile)

        slots = pl.ds(first, count)
        copy(("d", c), part.at[slots, pl.ds(theirs, 4)], swap_in.at[slots], other)

    def weight_terms(first, count, is_first, is_last):
        def tile(j):
            features = pl.ds(pl.multiple_of(j * TILE, TILE), TILE)
            tokens = xs[first : first + count, :, :, features].reshape(count * NZ * OWN, TILE)
            grads = gh[first : first + count].reshape(count * NZ * OWN, WIDTH)
            terms = lax.dot_general(
                tokens, grads, (((0,), (0,)), ((), ())), preferred_element_type=f32
            )
            if not is_first:
                terms = terms + gw[features, :]
            if is_last:
                terms = terms * factor
            gw[features, :] = terms

        each(WIDTH // TILE, tile)

    def both(slot, j):
        return part[slot, mine + j] + swap_in[slot, j]

    def swapped(c):
        arrived(("d", c))

    def x_first(dy):
        slot = slot_at(dy, 2)

        def one(j):
            x_out[dy, j // 2, 0, j] = both(slot, j).astype(bf16)

        each(4, one)
        for way in range(2):
            rows = pl.ds(2 * way, 2)
            copy(("e", dy, 0, way), x_out.at[dy, way, 0, rows], x_got.at[dy, way, 0, rows], first_near[way])

    def x_second(dy, way):
        slot = slot_at(dy, (1, 3)[way])
        arrived(("e", dy, 0, way))

        def with_got(j):
            j = j + 2 * way
            x_out[dy, way, 1, j] = (both(slot, j) + x_got[dy, way, 0, j].astype(f32)).astype(bf16)

        def without(j):
            j = j + 2 * (1 - way)
            x_out[dy, way, 1, j] = both(slot, j).astype(bf16)

        each(2, with_got)
        each(2, without)
        copy(("e", dy, 1, way), x_out.at[dy, way, 1], x_got.at[dy, way, 1], first_near[way])

    def x_last(dy):
        slot = slot_at(dy, 0)
        arrived(("e", dy, 1, 0))
        arrived(("e", dy, 1, 1))

        def one(j):
            total[dy, j] = (
                both(slot, j) + x_got[dy, 0, 1, j].astype(f32) + x_got[dy, 1, 1, j].astype(f32)
            )

        each(4, one)

    def y_first():
        def one(j):
            y_out[j // 2, 0, j] = total[2, j].astype(bf16)

        each(4, one)
        for way in range(2):
            rows = pl.ds(2 * way, 2)
            copy(("y", 0, way), y_out.at[way, 0, rows], y_got.at[way, 0, rows], second_near[way])

    def y_second(way):
        arrived(("y", 0, way))

        def with_got(j):
            j = j + 2 * way
            y_out[way, 1, j] = (total[(1, 3)[way], j] + y_got[way, 0, j].astype(f32)).astype(bf16)

        def without(j):
            j = j + 2 * (1 - way)
            y_out[way, 1, j] = total[(1, 3)[way], j].astype(bf16)

        each(2, with_got)
        each(2, without)
        copy(("y", 1, way), y_out.at[way, 1], y_got.at[way, 1], second_near[way])

    def y_last():
        arrived(("y", 1, 0))
        arrived(("y", 1, 1))

        def one(j):
            dx[j] = (
                total[0, j] + y_got[0, 1, j].astype(f32) + y_got[1, 1, j].astype(f32)
            ).astype(bf16)

        each(4, one)

    actions = dict(
        s=start, x=gather, k=spread_cot, m=forward, r=scatter, f=activate, g=spread, b=input_terms, t=turn,
        w=weight_terms, d=swapped, e=x_first, h=x_second, j=x_last, u=y_first, v=y_second, z=y_last,
    )
    sent = []
    done = 0
    for event in ORDER:
        actions[event[0]](*event[1:])
        sent.append(len(copies))
        if len(sent) > SEND_LAG:
            upto = sent[-1 - SEND_LAG]
            for made in list(copies.values())[done:upto]:
                made.wait_send()
            done = upto
    for slot in range(len(SLOTS)):
        if slot != SLOT[0, 0]:
            arrived(("a", slot))
    for made in list(copies.values())[done:]:
        made.wait_send()
    act_copy.wait()


def hand_over(act, dx, gw, act_out, dx_out, gw_out, sem):
    parts = [(act, act_out, pl.ds(0, OWN)), (dx, dx_out, pl.ds(0, 4))]
    parts += [(gw, gw_out, pl.ds(j * 96, 96)) for j in range(WIDTH // 96)]
    made = [
        pltpu.make_async_copy(src.at[rows], dst.at[rows], sem.at[i])
        for i, (src, dst, rows) in enumerate(parts)
    ]
    for one in made:
        one.start()
    for one in made:
        one.wait()


def local(inputs, weight, cotangent):
    slots = NY * NX
    factor = 1.0 / math.sqrt(slots * NZ * OWN)
    shapes = (
        pltpu.VMEM((OWN, slots * WIDTH), bf16),
        pltpu.VMEM((4, OWN, WIDTH), bf16),
        pltpu.VMEM((WIDTH, WIDTH), f32),
    )
    anywhere = [pl.BlockSpec(memory_space=pl.ANY)] * 3
    act, dx, gw = pl.pallas_call(
        functools.partial(kernel, factor),
        out_shape=shapes,
        in_specs=anywhere,
        out_specs=[pl.BlockSpec(memory_space=pltpu.VMEM)] * 3,
        scratch_shapes=[
            pltpu.VMEM((slots, NZ, OWN, WIDTH), bf16),
            pltpu.VMEM((slots, NZ, OWN, WIDTH), bf16),
            pltpu.VMEM((WIDTH, WIDTH), bf16),
            pltpu.VMEM((WIDTH, WIDTH), bf16),
            pltpu.VMEM((slots, OWN, WIDTH), bf16),
            pltpu.VMEM((slots, NZ, OWN, WIDTH), f32),
            pltpu.VMEM((2, 4, slots, OWN, WIDTH), bf16),
            pltpu.VMEM((2, 4, slots, OWN, WIDTH), bf16),
            pltpu.VMEM((slots, OWN, WIDTH), bf16),
            pltpu.VMEM((slots, 4, OWN, WIDTH), f32),
            pltpu.VMEM((NY, 2, 2, 4, OWN, WIDTH), bf16),
            pltpu.VMEM((NY, 2, 2, 4, OWN, WIDTH), bf16),
            pltpu.VMEM((NY, 4, OWN, WIDTH), f32),
            pltpu.VMEM((2, 2, 4, OWN, WIDTH), bf16),
            pltpu.VMEM((2, 2, 4, OWN, WIDTH), bf16),
            pltpu.SemaphoreType.DMA((COPIES,)),
            pltpu.SemaphoreType.DMA((COPIES,)),
            pltpu.SemaphoreType.DMA((4,)),
        ],
        compiler_params=pltpu.CompilerParams(
            collective_id=0, has_side_effects=True, vmem_limit_bytes=56 * 2**20
        ),
        cost_estimate=pl.CostEstimate(flops=7 * 10**9, bytes_accessed=10**7, transcendentals=2 * 10**5),
    )(inputs.reshape(4, OWN, WIDTH), weight[0], cotangent)
    act, dx, gw = pl.pallas_call(
        hand_over,
        out_shape=[jax.ShapeDtypeStruct(one.shape, one.dtype) for one in shapes],
        in_specs=anywhere,
        out_specs=anywhere,
        scratch_shapes=[pltpu.SemaphoreType.DMA((2 + WIDTH // 96,))],
    )(*(pltpu.with_memory_space_constraint(one, pltpu.VMEM) for one in (act, dx, gw)))
    return (act, dx.reshape(4 * OWN, WIDTH), gw[None])


def solution(mesh):
    in_specs = (P(("depth", "col"), "row"), P("col", "row", "depth"), P(("depth", "row"), "col"))
    out_specs = (P(("depth", "row"), "col"), P(("depth", "col"), "row"), P("col", "row", "depth"))
    return jax.shard_map(local, mesh=mesh, in_specs=in_specs, out_specs=out_specs, check_vma=False)
```
